512 devices in a mesh: row: 16 (over y_hi, x), col: 16 (over z, core), day: 2 (over y_lo).
Axes of the slice: x: 4, y: 8 (y_hi: 4, y_lo: 2; y = y_hi * 2 + y_lo), z: 8, core: 2. Of those that a mesh axis runs over, the one named last changes fastest.
Arguments:
- spectra: bfloat16 [2, 6, 1024, 512], P('day', None, ('row', 'col')), may hold values from -180 to 180
- avail: int32 [2, 6, 1024], P('day', None, ('row', 'col')), may hold values 0 or 1
Outputs:
- pws: bfloat16 [16, 16, 32, 64, 128], P('row', 'col', None, 'day')
The draws below stay inside these ranges and needn't reach their ends.
All inputs are finite; a program needn't handle non-finite values. No bound on the sum of `avail` on one device may be relied on, other than what follows from the above.
Results may differ from the reference program's by a relative error of at most 0.018.
Values may be sent and summed in bfloat16 or wider, within the bound.
No kernel may reach another device: no remote copies, remote signals or barrier semaphores. Data moves between devices by JAX's collectives and lax.ppermute only.
A program may use at most 64 MiB of HBM per device.

```python
import math
import jax
import jax.numpy as jnp
from jax import lax

BLOCK = 64
BINS = 256
LAGS = 128
HOURS = 6
DAY_DEV = 1
DAYS = 2
S = 1024
N_ROW = 16
N_COL = 16
N_DAY = 2


def draw_spectra(key, part):
    key = jax.random.fold_in(key, 7)
    key_base, key_station, key_band = jax.random.split(key, 3)
    shape = (DAYS, HOURS, S, 2 * BINS)
    base = jax.random.truncated_normal(key_base, -6.0, 6.0, shape, jnp.float32)
    top = math.log(10.0)
    station = jnp.exp(jax.random.uniform(key_station, (DAYS, HOURS, S, 1), jnp.float32, 0.0, top))
    band = jnp.exp(jax.random.uniform(key_band, (BINS,), jnp.float32, math.log(0.3), math.log(3.0)))
    values = base * station * jnp.concatenate([band, band])[None, None, None, :]
    return values.astype(jnp.bfloat16)


def with_ends(result, key, smallest, top_value):
    place = [jax.random.randint(jax.random.fold_in(key, axis), (), 0, length) for axis, length in enumerate(result.shape)]
    longest = result.shape.index(max(result.shape))
    beside = place[:longest] + [(place[longest] + 1) % result.shape[longest]] + place[longest + 1:]
    return result.at[tuple(place)].set(smallest).at[tuple(beside)].set(top_value)


def setup_inputs(seed: int = 0) -> dict:
    key_list = jax.random.split(jax.random.key(seed), 3)
    return {
        "spectra": draw_spectra(jax.random.fold_in(key_list[2], 71), 0),
        "avail": with_ends((jax.random.randint(key_list[1], (DAYS, HOURS, S), 0, 4) < 3).astype(jnp.int32), jax.random.fold_in(key_list[1], 1), 0, 1),
    }


def whiten(spectra, avail):
    values = spectra.astype(jnp.float32)
    bins = values.shape[-1] // 2
    power = values[..., :bins] ** 2 + values[..., bins:] ** 2
    level = lax.optimization_barrier(jnp.mean(power, axis=-1, keepdims=True)) + 1e-06
    factor = avail.astype(jnp.float32)[..., None] / jnp.sqrt(power + 0.09 * level)
    return (values * jnp.concatenate([factor, factor], axis=-1)).astype(jnp.bfloat16)

def lag_table(bins, lags, hours):
    freq = (jnp.arange(bins, dtype=jnp.float32) + 0.5) * (math.pi / bins)
    shifts = jnp.arange(lags, dtype=jnp.float32) - lags // 2
    angles = freq[:, None] * shifts[None, :]
    cosine = jnp.cos(angles)
    sine = jnp.sin(angles)
    upper = jnp.concatenate([cosine, sine], axis=1)
    lower = jnp.concatenate([-sine, cosine], axis=1)
    table = jnp.concatenate([upper, lower], axis=0) * (1.0 / math.sqrt(hours * bins))
    return table.astype(jnp.bfloat16)

def phasor_terms(cross, table):
    lags = table.shape[1] // 2
    flat = cross.reshape(-1, cross.shape[-1])
    both = jnp.dot(flat, table, preferred_element_type=jnp.float32)
    both = both.reshape(cross.shape[:-1] + (table.shape[1],))
    corr = both[..., :lags]
    hilb = both[..., lags:]
    amp = corr * corr + hilb * hilb
    spread = lax.optimization_barrier(jnp.mean(amp, axis=-1, keepdims=True)) + 1e-06
    inverse = 1.0 / jnp.sqrt(amp + 0.01 * spread)
    return (corr, both * jnp.concatenate([inverse, inverse], axis=-1))

def cross_spectrum(first, second):
    bins = first.shape[-1] // 2
    first = first.astype(jnp.float32)
    second = second.astype(jnp.float32)
    first_re, first_im = (first[..., :bins], first[..., bins:])
    second_re, second_im = (second[..., :bins], second[..., bins:])
    real_sum = jnp.einsum('hik,hjk->ijk', first_re, second_re) + jnp.einsum('hik,hjk->ijk', first_im, second_im)
    imag_sum = jnp.einsum('hik,hjk->ijk', first_im, second_re) - jnp.einsum('hik,hjk->ijk', first_re, second_im)
    return jnp.concatenate([real_sum, imag_sum], axis=-1).astype(jnp.bfloat16)

def mix_diagonal(cross, extra, same):
    half = extra.shape[0]
    bins = extra.shape[-1] // 2
    flipped = jnp.concatenate([extra[..., :bins], -extra[..., bins:]], axis=-1)
    rows_idx = jnp.arange(half, dtype=jnp.int32)[:, None, None]
    cols_idx = jnp.arange(half, dtype=jnp.int32)[None, :, None]
    left = cross[:, :half]
    zeros = jnp.zeros_like(left)
    left = jnp.where(rows_idx < cols_idx, left, jnp.where(rows_idx > cols_idx, flipped, zeros))
    mixed = jnp.concatenate([left, cross[:, half:]], axis=1)
    return jnp.where(same, mixed, cross)

def reference(spectra, avail):
    white = whiten(spectra, avail)
    table = lag_table(BINS, LAGS, HOURS)
    half = BLOCK // 2

    def one_position(position):
        row_id = position // N_COL
        col_id = position % N_COL
        low = jnp.minimum(row_id, col_id)
        high = jnp.maximum(row_id, col_id)
        first_start = (low * BLOCK + jnp.where(row_id > col_id, half, 0)).astype(jnp.int32)
        second_start = (high * BLOCK).astype(jnp.int32)
        bottom_start = (low * BLOCK + half).astype(jnp.int32)
        same = row_id == col_id
        firsts = lax.dynamic_slice_in_dim(white, first_start, half, 2)
        seconds = lax.dynamic_slice_in_dim(white, second_start, BLOCK, 2)
        bottoms = lax.dynamic_slice_in_dim(white, bottom_start, half, 2)
        lin_total = jnp.zeros((half, BLOCK, LAGS), jnp.float32)
        phase_total = jnp.zeros((half, BLOCK, 2 * LAGS), jnp.float32)
        for group in range(N_DAY):
            lin_part = jnp.zeros((half, BLOCK, LAGS), jnp.float32)
            phase_part = jnp.zeros((half, BLOCK, 2 * LAGS), jnp.float32)
            for inner in range(DAY_DEV):
                day_index = group * DAY_DEV + inner
                cross = cross_spectrum(firsts[day_index], seconds[day_index])
                extra = cross_spectrum(bottoms[day_index], bottoms[day_index])
                cross = mix_diagonal(cross, extra, same)
                corr, phase = phasor_terms(cross, table)
                lin_part = lin_part + corr
                phase_part = phase_part + phase
            lin_total = lin_total + lax.optimization_barrier(lin_part.astype(jnp.bfloat16)).astype(jnp.float32)
            phase_total = phase_total + lax.optimization_barrier(phase_part.astype(jnp.bfloat16)).astype(jnp.float32)
        coherence = phase_total[..., :LAGS] ** 2 + phase_total[..., LAGS:] ** 2
        return (lin_total * coherence / float(DAYS * DAYS)).astype(jnp.bfloat16)
    positions = jnp.arange(N_ROW * N_COL, dtype=jnp.int32)
    blocks = lax.map(one_position, positions)
    return blocks.reshape(N_ROW, N_COL, half, BLOCK, LAGS)
```

```python
import math

import jax
import jax.numpy as jnp
import ml_dtypes
import numpy as np
from jax import lax
from jax.experimental import pallas as pl
from jax.experimental.pallas import tpu as pltpu
from jax.sharding import PartitionSpec as P

BINS = 256
LAGS = 128
HOURS = 6
AXES = ("row", "col", "day")


def lag_table():
    freq = (np.arange(BINS) + 0.5) * (math.pi / BINS)
    angles = freq[:, None] * (np.arange(LAGS) - LAGS // 2)[None, :]
    upper = np.concatenate([np.cos(angles), np.sin(angles)], 1)
    lower = np.concatenate([-np.sin(angles), np.cos(angles)], 1)
    return (np.concatenate([upper, lower], 0) / math.sqrt(HOURS * BINS)).astype(ml_dtypes.bfloat16)

def whiten_kernel(spec_ref, avail_ref, out_ref, rows):
    eye = lax.broadcasted_iota(jnp.int32, (4, 4), 0) == lax.broadcasted_iota(jnp.int32, (4, 4), 1)
    avail = avail_ref[0].astype(jnp.float32)
    for h in range(HOURS):
        x = spec_ref[0, h].astype(jnp.float32)
        re, im = x[:, :BINS], x[:, BINS:]
        power = re * re + im * im
        level = jnp.mean(power, axis=1, keepdims=True) + 1e-06
        usable = jnp.sum(jnp.where(eye, avail[h:h + 1, :], 0.0), axis=1, keepdims=True)
        factor = usable * lax.rsqrt(power + 0.09 * level)
        white = (re * factor, im * factor)
        for part in range(4):
            piece = white[part // 2][:, (part % 2) * 128:(part % 2) * 128 + 128]
            rows[pl.ds(part * 24 + h, 4, stride=6), :] = piece
    out_ref[...] = rows[...].astype(jnp.bfloat16)

def whiten(spectra, avail):
    return pl.pallas_call(
        whiten_kernel,
        out_shape=jax.ShapeDtypeStruct((96, 128), jnp.bfloat16),
        scratch_shapes=[pltpu.VMEM((96, 128), jnp.float32)],
        name="whiten",
    )(spectra, avail)

def stack_kernel(place_ref, row_ref, col_ref, table_ref, out_ref, rows, firsts, seconds, cross, both):
    row_id = place_ref[0]
    col_id = place_ref[1]
    day_id = place_ref[2]
    below = row_id > col_id
    same = row_id == col_id
    corner = jnp.logical_and(same, day_id == 0)
    step = pl.program_id(0)

    def spread_first(day, j, block, slot):
        v = block.astype(jnp.float32)
        for part in range(4):
            firsts[slot, part, pl.ds(pl.multiple_of(day * 192 + j * 24, 8), 24), :] = v[part * 24:part * 24 + 24]

    def spread_second(day, j, block):
        v = block.astype(jnp.float32)
        for part in range(4):
            rows[part, pl.ds(pl.multiple_of(day * 192 + j * 24, 8), 24), :] = v[part * 24:part * 24 + 24]

    def split_hours(slot):
        for day in range(2):
            for h in range(HOURS):
                for part in range(4):
                    v = rows[part, pl.ds(day * 192 + h, 32, stride=6), :]
                    if slot == 1 and part >= 2:
                        v = -v
                    seconds[slot, day, h, part] = v

    @pl.when(step == 0)
    def _():
        for day in range(2):
            @pl.loop(0, 8)
            def _(j):
                @pl.when(below)
                def _():
                    spread_first(day, j, col_ref[j + 8, day], 0)
                    spread_second(day, j, row_ref[j + 8 * day_id, day])
                @pl.when(jnp.logical_not(below))
                def _():
                    spread_first(day, j, row_ref[j, day], 0)
                    @pl.when(same)
                    def _():
                        spread_second(day, j, row_ref[j + 8 * day_id, day])
                    @pl.when(jnp.logical_not(same))
                    def _():
                        spread_second(day, j, col_ref[j + 8 * day_id, day])
        split_hours(0)
        @pl.when(corner)
        def _():
            for day in range(2):
                @pl.loop(0, 8)
                def _(j):
                    v = row_ref[j + 8, day]
                    spread_second(day, j, v)
                    w = v.astype(jnp.float32)
                    for part in range(4):
                        piece = w[part * 24:part * 24 + 24]
                        firsts[1, part, pl.ds(pl.multiple_of(day * 192 + j * 24, 8), 24), :] = piece if part < 2 else -piece
            split_hours(1)

    def tile(src, day, a, q):
        acc = [None] * 4
        for h in range(HOURS):
            first = [firsts[src, part, pl.ds(day * 192 + a * 6 + h, 1), :] for part in range(4)]
            second = [seconds[src, day, h, part, pl.ds(q * 8, 8), :] for part in range(4)]
            for k in range(2):
                fr, fi = first[k], first[k + 2]
                sr, si = second[k], second[k + 2]
                re = fr * sr + fi * si
                im = fi * sr - fr * si
                acc[k] = re if h == 0 else acc[k] + re
                acc[k + 2] = im if h == 0 else acc[k + 2] + im
        return jnp.concatenate(acc, axis=1)

    @pl.loop(0, 8)
    def _(i):
        a = step * 8 + i
        for day in range(2):
            tiles = []
            for q in range(4):
                src = jnp.where(jnp.logical_and(corner, q < step), 1, 0)
                tiles.append(tile(src, day, a, q))
            cross[day, pl.ds(pl.multiple_of(i * 32, 32), 32), :] = jnp.concatenate(tiles, axis=0).astype(jnp.bfloat16)

    @pl.when(corner)
    def _():
        @pl.loop(0, 8)
        def _(i):
            a = step * 8 + i
            j = lax.broadcasted_iota(jnp.int32, (32, 512), 0)
            for day in range(2):
                other = tile(1, day, a, step)
                other = jnp.concatenate([other] * 4, axis=0)
                at = pl.ds(pl.multiple_of(i * 32, 32), 32)
                own = cross[day, at, :].astype(jnp.float32)
                inside = jnp.logical_and(j // 8 == step, j < a)
                own = jnp.where(inside, other, jnp.where(j == a, 0.0, own))
                cross[day, at, :] = own.astype(jnp.bfloat16)

    for day in range(2):
        both[day] = jnp.dot(cross[day], table_ref[...], preferred_element_type=jnp.float32)

    @pl.loop(0, 8)
    def _(i):
        at = pl.ds(pl.multiple_of(i * 32, 32), 32)
        lin = pr = pi = None
        for day in range(2):
            corr = both[day, at, :LAGS]
            hilb = both[day, at, LAGS:]
            amp = corr * corr + hilb * hilb
            spread = jnp.mean(amp, axis=1, keepdims=True) + 1e-06
            inverse = lax.rsqrt(amp + 0.01 * spread)
            if day == 0:
                lin, pr, pi = corr, corr * inverse, hilb * inverse
            else:
                lin, pr, pi = lin + corr, pr + corr * inverse, pi + hilb * inverse
        out_ref[i] = (lin * (pr * pr + pi * pi) * 0.25).astype(jnp.bfloat16)

def stack(place, row_side, col_side):
    table = jnp.asarray(lag_table())
    whole = lambda n: (lambda i: (0,) * n)
    return pl.pallas_call(
        stack_kernel,
        grid=(4,),
        in_specs=[
            pl.BlockSpec(memory_space=pltpu.SMEM),
            pl.BlockSpec((16, 2, 96, 128), whole(4)),
            pl.BlockSpec((16, 2, 96, 128), whole(4)),
            pl.BlockSpec((512, 256), whole(2)),
        ],
        out_specs=pl.BlockSpec((8, 32, 128), lambda i: (i, 0, 0)),
        out_shape=jax.ShapeDtypeStruct((32, 32, 128), jnp.bfloat16),
        scratch_shapes=[
            pltpu.VMEM((4, 384, 128), jnp.float32),
            pltpu.VMEM((2, 4, 384, 128), jnp.float32),
            pltpu.VMEM((2, 2, 6, 4, 32, 128), jnp.float32),
            pltpu.VMEM((2, 256, 512), jnp.bfloat16),
            pltpu.VMEM((2, 256, 256), jnp.float32),
        ],
        compiler_params=pltpu.CompilerParams(vmem_limit_bytes=32 * 1024 * 1024),
        name="stack",
    )(place, row_side, col_side, table)

def body(spectra, avail):
    n_row, n_col, n_day = (lax.axis_size(name) for name in AXES)
    place = jnp.stack([lax.axis_index(name) for name in AXES]).astype(jnp.int32)
    white = whiten(spectra, avail)
    pair = lax.all_gather(white, "day", axis=0)
    turn = [
        ((r * n_col + c) * n_day + d, (c * n_row + r) * n_day + d)
        for r in range(n_row) for c in range(n_col) for d in range(n_day)
    ]
    turned = lax.ppermute(pair, AXES, turn)
    col_side = lax.all_to_all(jnp.broadcast_to(turned[None], (n_row,) + turned.shape), "row", 0, 0, tiled=True)
    row_side = lax.all_gather(pair, "col", axis=0)
    return stack(place, row_side, col_side)[None, None]


def solution(mesh):
    placed = (P("day", None, ("row", "col"), None), P("day", None, ("row", "col")))
    return jax.shard_map(
        body,
        mesh=mesh,
        in_specs=placed,
        out_specs=P("row", "col", None, "day", None),
        check_vma=False,
    )
```

```python
import math

import jax
import jax.numpy as jnp
import ml_dtypes
import numpy as np
from jax import lax
from jax.experimental import pallas as pl
from jax.experimental.pallas import tpu as pltpu
from jax.sharding import PartitionSpec as P

BINS = 256
LAGS = 128
HOURS = 6
AXES = ("row", "col", "day")
DT = jnp.bfloat16
G = 16
CH = 32
UN = 4


def lag_table():
    freq = (np.arange(BINS) + 0.5) * (math.pi / BINS)
    angles = freq[:, None] * (np.arange(LAGS) - LAGS // 2)[None, :]
    upper = np.concatenate([np.cos(angles), np.sin(angles)], 1)
    lower = np.concatenate([-np.sin(angles), np.cos(angles)], 1)
    return (np.concatenate([upper, lower], 0) / math.sqrt(HOURS * BINS)).astype(ml_dtypes.bfloat16)

def whiten_kernel(spec_ref, avail_ref, out_ref, rows):
    avail = avail_ref[0].astype(jnp.float32)
    for h in range(HOURS):
        x = spec_ref[0, h].astype(jnp.float32)
        re, im = x[:, :BINS], x[:, BINS:]
        power = re * re + im * im
        level = jnp.mean(power, axis=1, keepdims=True) + 1e-06
        factor = avail[:, h:h + 1] * lax.rsqrt(power + 0.09 * level)
        white = (re * factor, im * factor)
        for part in range(4):
            piece = white[part // 2][:, (part % 2) * 128:(part % 2) * 128 + 128]
            rows[pl.ds(part * 24 + h, 4, stride=6), :] = piece
    out_ref[...] = rows[...].astype(jnp.bfloat16)

def whiten(spectra, avail):
    return pl.pallas_call(
        whiten_kernel,
        out_shape=jax.ShapeDtypeStruct((96, 128), jnp.bfloat16),
        scratch_shapes=[pltpu.VMEM((96, 128), jnp.float32)],
        name="whiten",
    )(spectra, avail.transpose(0, 2, 1))

def tree(terms):
    while len(terms) > 1:
        terms = [terms[i] + terms[i + 1] if i + 1 < len(terms) else terms[i] for i in range(0, len(terms), 2)]
    return terms[0]


def stack_kernel(place_ref, row_ref, col_ref, table_ref, out_ref, rows, firsts, seconds, cross):
    below = place_ref[0] > place_ref[1]
    day_id = place_ref[2]
    corner = jnp.logical_and(place_ref[0] == place_ref[1], day_id == 0)
    ones = jnp.full((LAGS, LAGS), 1.0, jnp.bfloat16)

    def split_hours(source):
        for day in range(2):
            for h in range(HOURS):
                for part in range(4):
                    v = rows[part, pl.ds(day * 192 + h, 32, stride=6), :]
                    if source == 1 and part >= 2:
                        v = -v
                    seconds[source, day, h, part] = v.astype(DT)

    @pl.loop(0, 8, unroll=2)
    def _(j):
        for day in range(2):
            at = pl.ds(pl.multiple_of(day * 192 + j * 24, 8), 24)
            first = jnp.where(below, col_ref[j + 8, day], row_ref[j, day]).astype(jnp.float32)
            second = jnp.where(below, row_ref[j + 8 * day_id, day], col_ref[j + 8 * day_id, day]).astype(jnp.float32)
            for part in range(4):
                firsts[part, at, :] = first[part * 24:part * 24 + 24]
                rows[part, at, :] = second[part * 24:part * 24 + 24]

    split_hours(0)

    @pl.when(corner)
    def _():
        @pl.loop(0, 8, unroll=2)
        def _(j):
            for day in range(2):
                at = pl.ds(pl.multiple_of(day * 192 + j * 24, 8), 24)
                first_at = pl.ds(pl.multiple_of(384 + day * 192 + j * 24, 8), 24)
                other = row_ref[j + 8, day].astype(jnp.float32)
                for part in range(4):
                    piece = other[part * 24:part * 24 + 24]
                    rows[part, at, :] = piece
                    firsts[part, first_at, :] = piece if part < 2 else -piece

        split_hours(1)

    def tile(source, day, a, q):
        at = source * 384 + day * 192 + a * 6
        parts = [None] * 4
        for k in range(2):
            re, im = [], []
            for h in range(HOURS):
                fr, fi = (
                    jnp.broadcast_to(firsts[part, pl.ds(at + h, 1), :], (G, 128)).astype(DT) for part in (k, k + 2)
                )
                sr, si = (seconds[source, day, h, part, q * G:(q + 1) * G, :] for part in (k, k + 2))
                re.append(fr * sr + fi * si)
                im.append(fi * sr - fr * si)
            parts[k], parts[k + 2] = tree(re), tree(im)
        return jnp.concatenate(parts, axis=1).astype(jnp.bfloat16)

    def fill(a, slot):
        for day in range(2):
            for q in range(32 // G):
                source = jnp.where(jnp.logical_and(corner, a // G > q), 1, 0)
                at = pl.ds(pl.multiple_of(slot * 32 + q * G, G), G)
                cross[day, at, :] = tile(source, day, a, q)

    def mend(a, slot):
        j = lax.broadcasted_iota(jnp.int32, (G, 512), 0)
        q = a // G
        inner = a - q * G
        for day in range(2):
            at = pl.ds(pl.multiple_of(slot * 32 + q * G, G), G)
            other = corner_tile(day, a, q).astype(jnp.float32)
            own = cross[day, at, :].astype(jnp.float32)
            own = jnp.where(j < inner, other, jnp.where(j == inner, 0.0, own))
            cross[day, at, :] = own.astype(jnp.bfloat16)

    def corner_tile(day, a, q):
        at = 384 + day * 192 + a * 6
        parts = [None] * 4
        for k in range(2):
            re, im = [], []
            for h in range(HOURS):
                fr, fi = (
                    jnp.broadcast_to(firsts[part, pl.ds(at + h, 1), :], (G, 128)).astype(DT) for part in (k, k + 2)
                )
                sr, si = (seconds[1, day, h, part, pl.ds(pl.multiple_of(q * G, G), G), :] for part in (k, k + 2))
                re.append(fr * sr + fi * si)
                im.append(fi * sr - fr * si)
            parts[k], parts[k + 2] = tree(re), tree(im)
        return jnp.concatenate(parts, axis=1).astype(jnp.bfloat16)

    def finish(a):
        table = table_ref[...]
        lin = re = im = None
        for day in range(2):
            both = jnp.dot(cross[day], table, preferred_element_type=jnp.float32)
            corr, hilb = both[:, :LAGS], both[:, LAGS:]
            amp = corr * corr + hilb * hilb
            spread = jnp.dot(amp.astype(jnp.bfloat16), ones, preferred_element_type=jnp.float32) * (1.0 / LAGS) + 1e-06
            inverse = lax.rsqrt(amp + 0.01 * spread)
            if day == 0:
                lin, re, im = corr, corr * inverse, hilb * inverse
            else:
                lin, re, im = lin + corr, re + corr * inverse, im + hilb * inverse
        stacked = (lin * (re * re + im * im) * 0.25).astype(jnp.bfloat16)
        out_ref[pl.ds(pl.multiple_of(a, CH), CH)] = stacked.reshape(CH, 32, LAGS)

    @pl.loop(0, 32 // CH)
    def _(i):
        @pl.loop(0, CH, unroll=UN)
        def _(slot):
            fill(i * CH + slot, slot)

        @pl.when(corner)
        def _():
            @pl.loop(0, CH, unroll=UN)
            def _(slot):
                mend(i * CH + slot, slot)

        finish(i * CH)


def stack(place, row_side, col_side):
    vmem = pl.BlockSpec(memory_space=pltpu.VMEM)
    return pl.pallas_call(
        stack_kernel,
        in_specs=[pl.BlockSpec(memory_space=pltpu.SMEM), vmem, vmem, vmem],
        out_specs=vmem,
        out_shape=jax.ShapeDtypeStruct((32, 32, LAGS), jnp.bfloat16),
        scratch_shapes=[
            pltpu.VMEM((4, 384, 128), jnp.float32),
            pltpu.VMEM((4, 768, 128), jnp.float32),
            pltpu.VMEM((2, 2, HOURS, 4, 32, 128), DT),
            pltpu.VMEM((2, CH * 32, 512), jnp.bfloat16),
        ],
        compiler_params=pltpu.CompilerParams(vmem_limit_bytes=32 * 1024 * 1024),
        name="stack",
    )(place, row_side, col_side, jnp.asarray(lag_table()))


def body(spectra, avail):
    n_row, n_col, n_day = (lax.axis_size(name) for name in AXES)
    place = jnp.stack([lax.axis_index(name) for name in AXES]).astype(jnp.int32)
    white = whiten(spectra, avail)
    pair = lax.all_gather(white, "day", axis=0)
    turn = [
        ((r * n_col + c) * n_day + d, (c * n_row + r) * n_day + d)
        for r in range(n_row) for c in range(n_col) for d in range(n_day)
    ]
    turned = lax.ppermute(pair, AXES, turn)
    col_side = lax.all_to_all(jnp.broadcast_to(turned[None], (n_row,) + turned.shape), "row", 0, 0, tiled=True)
    row_side = lax.all_gather(pair, "col", axis=0)
    return stack(place, row_side, col_side)[None, None]


def solution(mesh):
    placed = (P("day", None, ("row", "col"), None), P("day", None, ("row", "col")))
    return jax.shard_map(
        body,
        mesh=mesh,
        in_specs=placed,
        out_specs=P("row", "col", None, "day", None),
        check_vma=False,
    )
```

```python
import math

import jax
import jax.numpy as jnp
import ml_dtypes
import numpy as np
from jax import lax
from jax.experimental import pallas as pl
from jax.experimental.pallas import tpu as pltpu
from jax.sharding import PartitionSpec as P

BINS = 256
LAGS = 128
HOURS = 6
AXES = ("row", "col", "day")
DT = jnp.bfloat16
G = 16
CH = 32
UN = 8
UC = 4


def lag_table():
    freq = (np.arange(BINS) + 0.5) * (math.pi / BINS)
    angles = freq[:, None] * (np.arange(LAGS) - LAGS // 2)[None, :]
    upper = np.concatenate([np.cos(angles), np.sin(angles)], 1)
    lower = np.concatenate([-np.sin(angles), np.cos(angles)], 1)
    return (np.concatenate([upper, lower], 0) / math.sqrt(HOURS * BINS)).astype(ml_dtypes.bfloat16)

def whiten_kernel(spec_ref, avail_ref, out_ref, rows):
    avail = avail_ref[0].astype(jnp.float32)
    for h in range(HOURS):
        x = spec_ref[0, h].astype(jnp.float32)
        re, im = x[:, :BINS], x[:, BINS:]
        power = re * re + im * im
        level = jnp.mean(power, axis=1, keepdims=True) + 1e-06
        factor = avail[:, h:h + 1] * lax.rsqrt(power + 0.09 * level)
        white = (re * factor, im * factor)
        for part in range(4):
            piece = white[part // 2][:, (part % 2) * 128:(part % 2) * 128 + 128]
            rows[pl.ds(part * 24 + h, 4, stride=6), :] = piece
    out_ref[...] = rows[...].astype(jnp.bfloat16)

def whiten(spectra, avail):
    return pl.pallas_call(
        whiten_kernel,
        out_shape=jax.ShapeDtypeStruct((96, 128), jnp.bfloat16),
        scratch_shapes=[pltpu.VMEM((96, 128), jnp.float32)],
        name="whiten",
    )(spectra, avail.transpose(0, 2, 1))

def tree(terms):
    while len(terms) > 1:
        terms = [terms[i] + terms[i + 1] if i + 1 < len(terms) else terms[i] for i in range(0, len(terms), 2)]
    return terms[0]


def stack_kernel(place_ref, row_ref, col_ref, table_ref, out_ref, rows, firsts, seconds, cross):
    below = place_ref[0] > place_ref[1]
    above = place_ref[0] < place_ref[1]
    day_id = place_ref[2]
    corner = jnp.logical_and(place_ref[0] == place_ref[1], day_id == 0)
    ones = jnp.full((LAGS, LAGS), 1.0, jnp.bfloat16)

    def split_hours(source):
        for day in range(2):
            for h in range(HOURS):
                for part in range(4):
                    v = rows[part, pl.ds(day * 192 + h, 32, stride=6), :]
                    if source == 1 and part >= 2:
                        v = -v
                    seconds[source, day, h, part] = v.astype(DT)

    @pl.loop(0, 8, unroll=2)
    def _(j):
        for day in range(2):
            at = pl.ds(pl.multiple_of(day * 192 + j * 24, 8), 24)
            first = jnp.where(below, col_ref[2 * j + day], row_ref[j, day]).astype(jnp.float32)
            second = jnp.where(above, col_ref[2 * j + day], row_ref[j + 8 * day_id, day]).astype(jnp.float32)
            for part in range(4):
                firsts[part, at, :] = first[part * 24:part * 24 + 24]
                rows[part, at, :] = second[part * 24:part * 24 + 24]

    split_hours(0)

    @pl.when(corner)
    def _():
        @pl.loop(0, 8, unroll=2)
        def _(j):
            for day in range(2):
                at = pl.ds(pl.multiple_of(day * 192 + j * 24, 8), 24)
                first_at = pl.ds(pl.multiple_of(384 + day * 192 + j * 24, 8), 24)
                other = row_ref[j + 8, day].astype(jnp.float32)
                for part in range(4):
                    piece = other[part * 24:part * 24 + 24]
                    rows[part, at, :] = piece
                    firsts[part, first_at, :] = piece if part < 2 else -piece

        split_hours(1)

    def fill(a, plan):
        mark = lax.broadcasted_iota(jnp.int32, (G, 128), 0)
        inner = lax.rem(a, G)
        for day in range(2):
            parts = [[None] * 4 for _ in plan]
            for k in range(2):
                re, im = [[] for _ in plan], [[] for _ in plan]
                for h in range(HOURS):
                    at = day * 192 + a * 6 + h
                    wanted = sorted({s for p in plan for s in ((0, 1) if p is None else (p,))})
                    first = {
                        s: [
                            jnp.broadcast_to(firsts[part, pl.ds(s * 384 + at, 1), :], (G, 128)).astype(DT)
                            for part in (k, k + 2)
                        ]
                        for s in wanted
                    }
                    for q, p in enumerate(plan):
                        def second(s, part):
                            return seconds[s, day, h, part, q * G:(q + 1) * G, :]

                        if p is None:
                            fr, fi = (jnp.where(mark < inner, y, x) for x, y in zip(first[0], first[1]))
                            sr, si = (jnp.where(mark < inner, second(1, part), second(0, part)) for part in (k, k + 2))
                        else:
                            fr, fi = first[p]
                            sr, si = (second(p, part) for part in (k, k + 2))
                        re[q].append(fr * sr + fi * si)
                        im[q].append(fi * sr - fr * si)
                for q, p in enumerate(plan):
                    for part, terms in ((k, re[q]), (k + 2, im[q])):
                        total = tree(terms)
                        if p is None:
                            total = jnp.where(mark == inner, jnp.zeros_like(total), total)
                        at = pl.ds(pl.multiple_of(a * 32 + q * G, G), G)
                        cross[day, at, part * 128:part * 128 + 128] = total.astype(jnp.bfloat16)

    def finish(a):
        table = table_ref[...]
        lin = re = im = None
        for day in range(2):
            both = jnp.dot(cross[day], table, preferred_element_type=jnp.float32)
            corr, hilb = both[:, :LAGS], both[:, LAGS:]
            amp = corr * corr + hilb * hilb
            spread = jnp.dot(amp.astype(jnp.bfloat16), ones, preferred_element_type=jnp.float32) * (1.0 / LAGS) + 1e-06
            inverse = lax.rsqrt(amp + 0.01 * spread)
            if day == 0:
                lin, re, im = corr, corr * inverse, hilb * inverse
            else:
                lin, re, im = lin + corr, re + corr * inverse, im + hilb * inverse
        stacked = (lin * (re * re + im * im) * 0.25).astype(jnp.bfloat16)
        out_ref[pl.ds(pl.multiple_of(a, CH), CH)] = stacked.reshape(CH, 32, LAGS)

    @pl.when(corner)
    def _():
        @pl.loop(0, G, unroll=UC)
        def _(a):
            fill(a, (None, 0))

        @pl.loop(G, 2 * G, unroll=UC)
        def _(a):
            fill(a, (1, None))

    @pl.when(jnp.logical_not(corner))
    def _():
        @pl.loop(0, 32, unroll=UN)
        def _(a):
            fill(a, (0, 0))

    finish(0)


def stack(place, row_side, col_side):
    vmem = pl.BlockSpec(memory_space=pltpu.VMEM)
    return pl.pallas_call(
        stack_kernel,
        in_specs=[pl.BlockSpec(memory_space=pltpu.SMEM), vmem, vmem, vmem],
        out_specs=vmem,
        out_shape=jax.ShapeDtypeStruct((32, 32, LAGS), jnp.bfloat16),
        scratch_shapes=[
            pltpu.VMEM((4, 384, 128), jnp.float32),
            pltpu.VMEM((4, 768, 128), jnp.float32),
            pltpu.VMEM((2, 2, HOURS, 4, 32, 128), DT),
            pltpu.VMEM((2, CH * 32, 512), jnp.bfloat16),
        ],
        compiler_params=pltpu.CompilerParams(vmem_limit_bytes=32 * 1024 * 1024),
        name="stack",
    )(place, row_side, col_side, jnp.asarray(lag_table()))


def body(spectra, avail):
    n_row, n_col, n_day = (lax.axis_size(name) for name in AXES)
    row_id, col_id, day_id = place = [lax.axis_index(name) for name in AXES]
    white = whiten(spectra, avail)
    half = n_col // 2
    turn = [
        ((c * n_col + s) * n_day + day, ((s % half * n_day + day) * n_col + c) * n_day + s // half)
        for c in range(n_row) for s in range(n_col) for day in range(n_day)
    ]
    turned = lax.ppermute(white, AXES, turn)
    days = lax.all_gather(white, "day", axis=0)
    turned, days = lax.optimization_barrier((turned, days))
    halves = lax.all_gather(turned, "day", axis=0)
    upper = jnp.logical_or(lax.broadcasted_iota(jnp.int32, (n_row, 1, 1), 0) > col_id, day_id == 1)
    col_side = lax.all_to_all(jnp.where(upper, halves[1], halves[0]), "row", 0, 0, tiled=True)
    row_side = lax.all_gather(days, "col", axis=0)
    return stack(jnp.stack(place).astype(jnp.int32), row_side, col_side)[None, None]


def solution(mesh):
    placed = (P("day", None, ("row", "col"), None), P("day", None, ("row", "col")))
    return jax.shard_map(
        body,
        mesh=mesh,
        in_specs=placed,
        out_specs=P("row", "col", None, "day", None),
        check_vma=False,
    )
```

```python
import math

import jax
import jax.numpy as jnp
import ml_dtypes
import numpy as np
from jax import lax
from jax.experimental import pallas as pl
from jax.experimental.pallas import tpu as pltpu
from jax.sharding import PartitionSpec as P

BINS = 256
LAGS = 128
HOURS = 6
AXES = ("row", "col", "day")
MOVE = (11, 10, 14, 9, 13, 15, 3, 2, 0, 1, 4, 12, 6, 8, 5, 7)
DT = jnp.bfloat16
G = 16
CH = 32
UN = 8
UC = 4


def lag_table():
    freq = (np.arange(BINS) + 0.5) * (math.pi / BINS)
    angles = freq[:, None] * (np.arange(LAGS) - LAGS // 2)[None, :]
    upper = np.concatenate([np.cos(angles), np.sin(angles)], 1)
    lower = np.concatenate([-np.sin(angles), np.cos(angles)], 1)
    return (np.concatenate([upper, lower], 0) / math.sqrt(HOURS * BINS)).astype(ml_dtypes.bfloat16)

def whiten_kernel(spec_ref, avail_ref, out_ref, rows):
    avail = avail_ref[0].astype(jnp.float32)
    for h in range(HOURS):
        x = spec_ref[0, h].astype(jnp.float32)
        re, im = x[:, :BINS], x[:, BINS:]
        power = re * re + im * im
        level = jnp.mean(power, axis=1, keepdims=True) + 1e-06
        factor = avail[:, h:h + 1] * lax.rsqrt(power + 0.09 * level)
        white = (re * factor, im * factor)
        for part in range(4):
            piece = white[part // 2][:, (part % 2) * 128:(part % 2) * 128 + 128]
            rows[pl.ds(part * 24 + h, 4, stride=6), :] = piece
    out_ref[...] = rows[...].astype(jnp.bfloat16)

def whiten(spectra, avail):
    return pl.pallas_call(
        whiten_kernel,
        out_shape=jax.ShapeDtypeStruct((96, 128), jnp.bfloat16),
        scratch_shapes=[pltpu.VMEM((96, 128), jnp.float32)],
        name="whiten",
    )(spectra, avail.transpose(0, 2, 1))

def tree(terms):
    while len(terms) > 1:
        terms = [terms[i] + terms[i + 1] if i + 1 < len(terms) else terms[i] for i in range(0, len(terms), 2)]
    return terms[0]


def stack_kernel(place_ref, row_ref, col_ref, table_ref, out_ref, rows, firsts, seconds, cross):
    below = place_ref[0] > place_ref[1]
    above = place_ref[0] < place_ref[1]
    day_id = place_ref[2]
    col_start = jnp.where(above, 8 * day_id, 8)
    corner = jnp.logical_and(place_ref[0] == place_ref[1], day_id == 0)
    ones = jnp.full((LAGS, LAGS), 1.0, jnp.bfloat16)

    def held(shard):
        move = shard ^ place_ref[1]
        words = [sum(m << 4 * i for i, m in enumerate(MOVE[at:at + 8])) for at in (0, 8)]
        word = jnp.where(move < 8, words[0], words[1])
        return (lax.shift_right_logical(word, 4 * (move & 7)) & 15) ^ place_ref[1]

    def split_hours(source):
        for day in range(2):
            for h in range(HOURS):
                for part in range(4):
                    v = rows[part, pl.ds(day * 192 + h, 32, stride=6), :]
                    if source == 1 and part >= 2:
                        v = -v
                    seconds[source, day, h, part] = v.astype(DT)

    @pl.loop(0, 8, unroll=2)
    def _(j):
        for day in range(2):
            at = pl.ds(pl.multiple_of(day * 192 + j * 24, 8), 24)
            from_col = col_ref[held(col_start + j), day]
            first = jnp.where(below, from_col, row_ref[j, day]).astype(jnp.float32)
            second = jnp.where(above, from_col, row_ref[j + 8 * day_id, day]).astype(jnp.float32)
            for part in range(4):
                firsts[part, at, :] = first[part * 24:part * 24 + 24]
                rows[part, at, :] = second[part * 24:part * 24 + 24]

    split_hours(0)

    @pl.when(corner)
    def _():
        @pl.loop(0, 8, unroll=2)
        def _(j):
            for day in range(2):
                at = pl.ds(pl.multiple_of(day * 192 + j * 24, 8), 24)
                first_at = pl.ds(pl.multiple_of(384 + day * 192 + j * 24, 8), 24)
                other = row_ref[j + 8, day].astype(jnp.float32)
                for part in range(4):
                    piece = other[part * 24:part * 24 + 24]
                    rows[part, at, :] = piece
                    firsts[part, first_at, :] = piece if part < 2 else -piece

        split_hours(1)

    def fill(a, plan):
        mark = lax.broadcasted_iota(jnp.int32, (G, 128), 0)
        inner = lax.rem(a, G)
        for day in range(2):
            parts = [[None] * 4 for _ in plan]
            for k in range(2):
                re, im = [[] for _ in plan], [[] for _ in plan]
                for h in range(HOURS):
                    at = day * 192 + a * 6 + h
                    wanted = sorted({s for p in plan for s in ((0, 1) if p is None else (p,))})
                    first = {
                        s: [
                            jnp.broadcast_to(firsts[part, pl.ds(s * 384 + at, 1), :], (G, 128)).astype(DT)
                            for part in (k, k + 2)
                        ]
                        for s in wanted
                    }
                    for q, p in enumerate(plan):
                        def second(s, part):
                            return seconds[s, day, h, part, q * G:(q + 1) * G, :]

                        if p is None:
                            fr, fi = (jnp.where(mark < inner, y, x) for x, y in zip(first[0], first[1]))
                            sr, si = (jnp.where(mark < inner, second(1, part), second(0, part)) for part in (k, k + 2))
                        else:
                            fr, fi = first[p]
                            sr, si = (second(p, part) for part in (k, k + 2))
                        re[q].append(fr * sr + fi * si)
                        im[q].append(fi * sr - fr * si)
                for q, p in enumerate(plan):
                    for part, terms in ((k, re[q]), (k + 2, im[q])):
                        total = tree(terms)
                        if p is None:
                            total = jnp.where(mark == inner, jnp.zeros_like(total), total)
                        at = pl.ds(pl.multiple_of(a * 32 + q * G, G), G)
                        cross[day, at, part * 128:part * 128 + 128] = total.astype(jnp.bfloat16)

    def finish(a):
        table = table_ref[...]
        lin = re = im = None
        for day in range(2):
            both = jnp.dot(cross[day], table, preferred_element_type=jnp.float32)
            corr, hilb = both[:, :LAGS], both[:, LAGS:]
            amp = corr * corr + hilb * hilb
            spread = jnp.dot(amp.astype(jnp.bfloat16), ones, preferred_element_type=jnp.float32) * (1.0 / LAGS) + 1e-06
            inverse = lax.rsqrt(amp + 0.01 * spread)
            if day == 0:
                lin, re, im = corr, corr * inverse, hilb * inverse
            else:
                lin, re, im = lin + corr, re + corr * inverse, im + hilb * inverse
        stacked = (lin * (re * re + im * im) * 0.25).astype(jnp.bfloat16)
        out_ref[pl.ds(pl.multiple_of(a, CH), CH)] = stacked.reshape(CH, 32, LAGS)

    @pl.when(corner)
    def _():
        @pl.loop(0, G, unroll=UC)
        def _(a):
            fill(a, (None, 0))

        @pl.loop(G, 2 * G, unroll=UC)
        def _(a):
            fill(a, (1, None))

    @pl.when(jnp.logical_not(corner))
    def _():
        @pl.loop(0, 32, unroll=UN)
        def _(a):
            fill(a, (0, 0))

    finish(0)


def stack(place, row_side, col_side):
    vmem = pl.BlockSpec(memory_space=pltpu.VMEM)
    return pl.pallas_call(
        stack_kernel,
        in_specs=[pl.BlockSpec(memory_space=pltpu.SMEM), vmem, vmem, vmem],
        out_specs=vmem,
        out_shape=jax.ShapeDtypeStruct((32, 32, LAGS), jnp.bfloat16),
        scratch_shapes=[
            pltpu.VMEM((4, 384, 128), jnp.float32),
            pltpu.VMEM((4, 768, 128), jnp.float32),
            pltpu.VMEM((2, 2, HOURS, 4, 32, 128), DT),
            pltpu.VMEM((2, CH * 32, 512), jnp.bfloat16),
        ],
        compiler_params=pltpu.CompilerParams(vmem_limit_bytes=32 * 1024 * 1024),
        name="stack",
    )(place, row_side, col_side, jnp.asarray(lag_table()))


def body(spectra, avail):
    n_row, n_col, n_day = (lax.axis_size(name) for name in AXES)
    row_id, col_id, day_id = (lax.axis_index(name) for name in AXES)
    white = whiten(spectra, avail)
    turn = [
        ((c * n_col + s) * n_day + day, ((c ^ MOVE[s ^ c]) * n_col + c) * n_day + day)
        for c in range(n_row) for s in range(n_col) for day in range(n_day)
    ]
    turned = lax.ppermute(white, AXES, turn)
    days = lax.all_gather(white, "day", axis=0)
    turned, days = lax.optimization_barrier((turned, days))
    pieces = jnp.broadcast_to(turned[None], (n_row * n_day,) + turned.shape)
    col_side = lax.all_to_all(pieces, ("row", "day"), 0, 0, tiled=True).reshape((n_row, n_day) + turned.shape)
    row_side = lax.all_gather(days, "col", axis=0)
    place = jnp.stack([row_id, col_id, day_id]).astype(jnp.int32)
    return stack(place, row_side, col_side)[None, None]


def solution(mesh):
    placed = (P("day", None, ("row", "col"), None), P("day", None, ("row", "col")))
    return jax.shard_map(
        body,
        mesh=mesh,
        in_specs=placed,
        out_specs=P("row", "col", None, "day", None),
        check_vma=False,
    )
```

```python
import math

import jax
import jax.numpy as jnp
import ml_dtypes
import numpy as np
from jax import lax
from jax.experimental import pallas as pl
from jax.experimental.pallas import tpu as pltpu
from jax.sharding import PartitionSpec as P

BINS = 256
LAGS = 128
HOURS = 6
AXES = ("row", "col", "day")
MOVE = (11, 10, 14, 9, 13, 15, 3, 2, 0, 1, 4, 12, 6, 8, 5, 7)
DT = jnp.bfloat16
G = 16
CH = 32
UN = 8
UC = 8


def lag_table():
    freq = (np.arange(BINS) + 0.5) * (math.pi / BINS)
    angles = freq[:, None] * (np.arange(LAGS) - LAGS // 2)[None, :]
    upper = np.concatenate([np.cos(angles), np.sin(angles)], 1)
    lower = np.concatenate([-np.sin(angles), np.cos(angles)], 1)
    return (np.concatenate([upper, lower], 0) / math.sqrt(HOURS * BINS)).astype(ml_dtypes.bfloat16)

def whiten_kernel(spec_ref, avail_ref, out_ref, rows):
    avail = avail_ref[0].astype(jnp.float32)
    for h in range(HOURS):
        x = spec_ref[0, h].astype(jnp.float32)
        re, im = x[:, :BINS], x[:, BINS:]
        power = re * re + im * im
        level = jnp.mean(power, axis=1, keepdims=True) + 1e-06
        factor = avail[:, h:h + 1] * lax.rsqrt(power + 0.09 * level)
        white = (re * factor, im * factor)
        for part in range(4):
            piece = white[part // 2][:, (part % 2) * 128:(part % 2) * 128 + 128]
            rows[pl.ds(part * 24 + h, 4, stride=6), :] = piece
    out_ref[...] = rows[...].astype(jnp.bfloat16)

def whiten(spectra, avail):
    return pl.pallas_call(
        whiten_kernel,
        out_shape=jax.ShapeDtypeStruct((96, 128), jnp.bfloat16),
        scratch_shapes=[pltpu.VMEM((96, 128), jnp.float32)],
        name="whiten",
    )(spectra, avail.transpose(0, 2, 1))

def tree(terms):
    while len(terms) > 1:
        terms = [terms[i] + terms[i + 1] if i + 1 < len(terms) else terms[i] for i in range(0, len(terms), 2)]
    return terms[0]


def stack_kernel(row_ref, col_ref, table_ref, out_ref, rows, firsts, seconds, cross):
    row_id, col_id, day_id = (lax.axis_index(name) for name in AXES)
    below = row_id > col_id
    above = row_id < col_id
    col_start = jnp.where(above, 8 * day_id, 8)
    corner = jnp.logical_and(row_id == col_id, day_id == 0)

    def held(shard):
        move = shard ^ col_id
        words = [sum(m << 4 * i for i, m in enumerate(MOVE[at:at + 8])) for at in (0, 8)]
        word = jnp.where(move < 8, words[0], words[1])
        return (lax.shift_right_logical(word, 4 * (move & 7)) & 15) ^ col_id

    def split_hours(source):
        for day in range(2):
            for h in range(HOURS):
                for part in range(4):
                    v = rows[part, pl.ds(day * 192 + h, 32, stride=6), :]
                    if source == 1 and part >= 2:
                        v = -v
                    seconds[source, day, h, part] = v.astype(DT)

    @pl.loop(0, 8, unroll=2)
    def _(j):
        for day in range(2):
            at = pl.ds(pl.multiple_of(day * 192 + j * 24, 8), 24)
            from_col = col_ref[held(col_start + j), day]
            first = jnp.where(below, from_col, row_ref[j, day]).astype(jnp.float32)
            second = jnp.where(above, from_col, row_ref[j + 8 * day_id, day]).astype(jnp.float32)
            for part in range(4):
                firsts[part, at, :] = first[part * 24:part * 24 + 24]
                rows[part, at, :] = second[part * 24:part * 24 + 24]

    split_hours(0)

    @pl.when(corner)
    def _():
        @pl.loop(0, 8, unroll=2)
        def _(j):
            for day in range(2):
                at = pl.ds(pl.multiple_of(day * 192 + j * 24, 8), 24)
                first_at = pl.ds(pl.multiple_of(384 + day * 192 + j * 24, 8), 24)
                other = row_ref[j + 8, day].astype(jnp.float32)
                for part in range(4):
                    piece = other[part * 24:part * 24 + 24]
                    rows[part, at, :] = piece
                    firsts[part, first_at, :] = piece if part < 2 else -piece

        split_hours(1)

    def fill(a, plan):
        mark = lax.broadcasted_iota(jnp.int16, (G, 128), 0)
        inner = jnp.full((G, 128), lax.rem(a, G), jnp.int32).astype(jnp.int16)
        for day in range(2):
            parts = [[None] * 4 for _ in plan]
            for k in range(2):
                re, im = [[] for _ in plan], [[] for _ in plan]
                for h in range(HOURS):
                    at = day * 192 + a * 6 + h
                    wanted = sorted({s for p in plan for s in ((0, 1) if p is None else (p,))})
                    first = {
                        s: [
                            jnp.broadcast_to(firsts[part, pl.ds(s * 384 + at, 1), :], (G, 128)).astype(DT)
                            for part in (k, k + 2)
                        ]
                        for s in wanted
                    }
                    for q, p in enumerate(plan):
                        def second(s, part):
                            return seconds[s, day, h, part, q * G:(q + 1) * G, :]

                        if p is None:
                            fr, fi = (jnp.where(mark < inner, y, x) for x, y in zip(first[0], first[1]))
                            sr, si = (jnp.where(mark < inner, second(1, part), second(0, part)) for part in (k, k + 2))
                        else:
                            fr, fi = first[p]
                            sr, si = (second(p, part) for part in (k, k + 2))
                        re[q].append(fr * sr + fi * si)
                        im[q].append(fi * sr - fr * si)
                for q, p in enumerate(plan):
                    for part, terms in ((k, re[q]), (k + 2, im[q])):
                        total = tree(terms)
                        if p is None:
                            total = jnp.where(mark == inner, jnp.zeros_like(total), total)
                        at = pl.ds(pl.multiple_of(a * 32 + q * G, G), G)
                        cross[day, at, part * 128:part * 128 + 128] = total.astype(jnp.bfloat16)

    def finish(a):
        table = table_ref[...]
        lin = re = im = None
        for day in range(2):
            both = jnp.dot(cross[day], table, preferred_element_type=jnp.float32)
            corr, hilb = both[:, :LAGS], both[:, LAGS:]
            amp = corr * corr + hilb * hilb
            spread = jnp.sum(amp, axis=1, keepdims=True) * (0.01 / LAGS) + 1e-08
            inverse = lax.rsqrt(amp + spread)
            if day == 0:
                lin, re, im = corr, corr * inverse, hilb * inverse
            else:
                lin, re, im = lin + corr, re + corr * inverse, im + hilb * inverse
        stacked = (lin * (re * re + im * im) * 0.25).astype(jnp.bfloat16)
        out_ref[pl.ds(pl.multiple_of(a, CH), CH)] = stacked.reshape(CH, 32, LAGS)

    @pl.when(corner)
    def _():
        @pl.loop(0, G, unroll=UC)
        def _(a):
            fill(a, (None, 0))

        @pl.loop(G, 2 * G, unroll=UC)
        def _(a):
            fill(a, (1, None))

    @pl.when(jnp.logical_not(corner))
    def _():
        @pl.loop(0, 32, unroll=UN)
        def _(a):
            fill(a, (0, 0))

    finish(0)


def stack(row_side, col_side):
    vmem = pl.BlockSpec(memory_space=pltpu.VMEM)
    return pl.pallas_call(
        stack_kernel,
        in_specs=[vmem, vmem, vmem],
        out_specs=vmem,
        out_shape=jax.ShapeDtypeStruct((32, 32, LAGS), jnp.bfloat16),
        scratch_shapes=[
            pltpu.VMEM((4, 384, 128), jnp.float32),
            pltpu.VMEM((4, 768, 128), jnp.float32),
            pltpu.VMEM((2, 2, HOURS, 4, 32, 128), DT),
            pltpu.VMEM((2, CH * 32, 512), jnp.bfloat16),
        ],
        compiler_params=pltpu.CompilerParams(vmem_limit_bytes=32 * 1024 * 1024),
        name="stack",
    )(row_side, col_side, jnp.asarray(lag_table()))


def body(spectra, avail):
    n_row, n_col, n_day = (lax.axis_size(name) for name in AXES)
    white = whiten(spectra, avail)
    turn = [
        ((c * n_col + s) * n_day + day, ((c ^ MOVE[s ^ c]) * n_col + c) * n_day + day)
        for c in range(n_row) for s in range(n_col) for day in range(n_day)
    ]
    turned = lax.ppermute(white, AXES, turn)
    days = lax.all_gather(white, "day", axis=0)
    turned, days = lax.optimization_barrier((turned, days))
    pieces = jnp.broadcast_to(turned[None], (n_row * n_day,) + turned.shape)
    col_side = lax.all_to_all(pieces, ("row", "day"), 0, 0, tiled=True).reshape((n_row, n_day) + turned.shape)
    row_side = lax.all_gather(days, "col", axis=0)
    return stack(row_side, col_side)[None, None]


def solution(mesh):
    placed = (P("day", None, ("row", "col"), None), P("day", None, ("row", "col")))
    return jax.shard_map(
        body,
        mesh=mesh,
        in_specs=placed,
        out_specs=P("row", "col", None, "day", None),
        check_vma=False,
    )
```

```python
import math

import jax
import jax.numpy as jnp
import ml_dtypes
import numpy as np
from jax import lax
from jax.experimental import pallas as pl
from jax.experimental.pallas import tpu as pltpu
from jax.sharding import PartitionSpec as P

BINS = 256
LAGS = 128
HOURS = 6
AXES = ("row", "col", "day")
HOLDER = (
    (11, 5, 6, 8, 10, 9, 13, 14, 7, 15, 0, 12, 3, 4, 1, 2),
    (4, 6, 9, 8, 11, 10, 7, 15, 14, 12, 1, 2, 5, 13, 0, 3),
    (7, 4, 10, 11, 8, 5, 9, 12, 13, 15, 2, 14, 3, 6, 1, 0),
    (12, 5, 8, 9, 6, 4, 11, 10, 14, 13, 3, 15, 1, 7, 2, 0),
    (1, 3, 2, 12, 14, 13, 15, 9, 11, 10, 0, 8, 7, 6, 4, 5),
    (2, 0, 8, 3, 12, 15, 14, 10, 11, 13, 9, 1, 6, 7, 5, 4),
    (2, 5, 1, 4, 3, 0, 13, 14, 15, 12, 11, 8, 10, 9, 6, 7),
    (3, 4, 5, 0, 1, 2, 13, 14, 8, 12, 15, 9, 11, 10, 7, 6),
    (8, 4, 0, 1, 2, 3, 7, 5, 14, 12, 15, 6, 9, 13, 11, 10),
    (1, 5, 2, 0, 4, 3, 6, 7, 15, 12, 13, 14, 8, 11, 9, 10),
    (3, 1, 5, 2, 4, 0, 6, 7, 8, 12, 14, 13, 11, 15, 10, 9),
    (1, 0, 4, 3, 5, 2, 8, 6, 7, 12, 14, 13, 9, 15, 11, 10),
    (15, 5, 3, 2, 0, 1, 12, 8, 13, 4, 6, 7, 10, 11, 9, 14),
    (4, 7, 3, 2, 1, 0, 5, 6, 8, 12, 9, 13, 10, 11, 15, 14),
    (6, 7, 4, 5, 0, 1, 3, 2, 8, 12, 15, 13, 9, 14, 11, 10),
    (5, 6, 4, 7, 2, 0, 1, 3, 12, 8, 15, 14, 13, 9, 10, 11),
)
DT = jnp.bfloat16
G = 16
CH = 32
UN = 8
UC = 8


def lag_table():
    freq = (np.arange(BINS) + 0.5) * (math.pi / BINS)
    angles = freq[:, None] * (np.arange(LAGS) - LAGS // 2)[None, :]
    upper = np.concatenate([np.cos(angles), np.sin(angles)], 1)
    lower = np.concatenate([-np.sin(angles), np.cos(angles)], 1)
    return (np.concatenate([upper, lower], 0) / math.sqrt(HOURS * BINS)).astype(ml_dtypes.bfloat16)

def whiten_kernel(spec_ref, avail_ref, out_ref, rows):
    avail = avail_ref[0].astype(jnp.float32)
    for h in range(HOURS):
        x = spec_ref[0, h].astype(jnp.float32)
        re, im = x[:, :BINS], x[:, BINS:]
        power = re * re + im * im
        level = jnp.mean(power, axis=1, keepdims=True) + 1e-06
        factor = avail[:, h:h + 1] * lax.rsqrt(power + 0.09 * level)
        white = (re * factor, im * factor)
        for part in range(4):
            piece = white[part // 2][:, (part % 2) * 128:(part % 2) * 128 + 128]
            rows[pl.ds(part * 24 + h, 4, stride=6), :] = piece
    out_ref[...] = rows[...].astype(jnp.bfloat16)

def whiten(spectra, avail):
    return pl.pallas_call(
        whiten_kernel,
        out_shape=jax.ShapeDtypeStruct((96, 128), jnp.bfloat16),
        scratch_shapes=[pltpu.VMEM((96, 128), jnp.float32)],
        name="whiten",
    )(spectra, avail.transpose(0, 2, 1))

def tree(terms):
    while len(terms) > 1:
        terms = [terms[i] + terms[i + 1] if i + 1 < len(terms) else terms[i] for i in range(0, len(terms), 2)]
    return terms[0]


def stack_kernel(row_ref, col_ref, table_ref, out_ref, rows, firsts, seconds, cross):
    row_id, col_id, day_id = (lax.axis_index(name) for name in AXES)
    below = row_id > col_id
    above = row_id < col_id
    col_start = jnp.where(above, 8 * day_id, 8)
    corner = jnp.logical_and(row_id == col_id, day_id == 0)

    def held(shard):
        word = jnp.int32(0)
        for column in range(16):
            words = [np.uint32(sum(k << 4 * i for i, k in enumerate(HOLDER[column][at:at + 8]))).astype(np.int32) for at in (0, 8)]
            word = jnp.where(col_id == column, jnp.where(shard < 8, words[0], words[1]), word)
        return lax.shift_right_logical(word, 4 * (shard & 7)) & 15

    def split_hours(source):
        for day in range(2):
            for h in range(HOURS):
                for part in range(4):
                    v = rows[part, pl.ds(day * 192 + h, 32, stride=6), :]
                    if source == 1 and part >= 2:
                        v = -v
                    seconds[source, day, h, part] = v.astype(DT)

    @pl.loop(0, 8, unroll=2)
    def _(j):
        holder = held(col_start + j)
        for day in range(2):
            at = pl.ds(pl.multiple_of(day * 192 + j * 24, 8), 24)
            from_col = col_ref[holder, day]
            first = jnp.where(below, from_col, row_ref[j, day]).astype(jnp.float32)
            second = jnp.where(above, from_col, row_ref[j + 8 * day_id, day]).astype(jnp.float32)
            for part in range(4):
                firsts[part, at, :] = first[part * 24:part * 24 + 24]
                rows[part, at, :] = second[part * 24:part * 24 + 24]

    split_hours(0)

    @pl.when(corner)
    def _():
        @pl.loop(0, 8, unroll=2)
        def _(j):
            for day in range(2):
                at = pl.ds(pl.multiple_of(day * 192 + j * 24, 8), 24)
                first_at = pl.ds(pl.multiple_of(384 + day * 192 + j * 24, 8), 24)
                other = row_ref[j + 8, day].astype(jnp.float32)
                for part in range(4):
                    piece = other[part * 24:part * 24 + 24]
                    rows[part, at, :] = piece
                    firsts[part, first_at, :] = piece if part < 2 else -piece

        split_hours(1)

    def fill(a, plan):
        mark = lax.broadcasted_iota(jnp.int16, (G, 128), 0)
        inner = jnp.full((G, 128), lax.rem(a, G), jnp.int32).astype(jnp.int16)
        for day in range(2):
            parts = [[None] * 4 for _ in plan]
            for k in range(2):
                re, im = [[] for _ in plan], [[] for _ in plan]
                for h in range(HOURS):
                    at = day * 192 + a * 6 + h
                    wanted = sorted({s for p in plan for s in ((0, 1) if p is None else (p,))})
                    first = {
                        s: [
                            jnp.broadcast_to(firsts[part, pl.ds(s * 384 + at, 1), :], (G, 128)).astype(DT)
                            for part in (k, k + 2)
                        ]
                        for s in wanted
                    }
                    for q, p in enumerate(plan):
                        def second(s, part):
                            return seconds[s, day, h, part, q * G:(q + 1) * G, :]

                        if p is None:
                            fr, fi = (jnp.where(mark < inner, y, x) for x, y in zip(first[0], first[1]))
                            sr, si = (jnp.where(mark < inner, second(1, part), second(0, part)) for part in (k, k + 2))
                        else:
                            fr, fi = first[p]
                            sr, si = (second(p, part) for part in (k, k + 2))
                        re[q].append(fr * sr + fi * si)
                        im[q].append(fi * sr - fr * si)
                for q, p in enumerate(plan):
                    for part, terms in ((k, re[q]), (k + 2, im[q])):
                        total = tree(terms)
                        if p is None:
                            total = jnp.where(mark == inner, jnp.zeros_like(total), total)
                        at = pl.ds(pl.multiple_of(a * 32 + q * G, G), G)
                        cross[day, at, part * 128:part * 128 + 128] = total.astype(jnp.bfloat16)

    def finish(a):
        table = table_ref[...]
        lin = re = im = None
        for day in range(2):
            both = jnp.dot(cross[day], table, preferred_element_type=jnp.float32)
            corr, hilb = both[:, :LAGS], both[:, LAGS:]
            amp = corr * corr + hilb * hilb
            spread = jnp.sum(amp, axis=1, keepdims=True) * (0.01 / LAGS) + 1e-08
            inverse = lax.rsqrt(amp + spread)
            if day == 0:
                lin, re, im = corr, corr * inverse, hilb * inverse
            else:
                lin, re, im = lin + corr, re + corr * inverse, im + hilb * inverse
        stacked = (lin * (re * re + im * im) * 0.25).astype(jnp.bfloat16)
        out_ref[pl.ds(pl.multiple_of(a, CH), CH)] = stacked.reshape(CH, 32, LAGS)

    @pl.when(corner)
    def _():
        @pl.loop(0, G, unroll=UC)
        def _(a):
            fill(a, (None, 0))

        @pl.loop(G, 2 * G, unroll=UC)
        def _(a):
            fill(a, (1, None))

    @pl.when(jnp.logical_not(corner))
    def _():
        @pl.loop(0, 32, unroll=UN)
        def _(a):
            fill(a, (0, 0))

    finish(0)


def stack(row_side, col_side):
    vmem = pl.BlockSpec(memory_space=pltpu.VMEM)
    return pl.pallas_call(
        stack_kernel,
        in_specs=[vmem, vmem, vmem],
        out_specs=vmem,
        out_shape=jax.ShapeDtypeStruct((32, 32, LAGS), jnp.bfloat16),
        scratch_shapes=[
            pltpu.VMEM((4, 384, 128), jnp.float32),
            pltpu.VMEM((4, 768, 128), jnp.float32),
            pltpu.VMEM((2, 2, HOURS, 4, 32, 128), DT),
            pltpu.VMEM((2, CH * 32, 512), jnp.bfloat16),
        ],
        compiler_params=pltpu.CompilerParams(vmem_limit_bytes=32 * 1024 * 1024),
        name="stack",
    )(row_side, col_side, jnp.asarray(lag_table()))


def body(spectra, avail):
    n_row, n_col, n_day = (lax.axis_size(name) for name in AXES)
    white = whiten(spectra, avail)
    turn = [
        ((c * n_col + s) * n_day + day, (HOLDER[c][s] * n_col + c) * n_day + day)
        for c in range(n_row) for s in range(n_col) for day in range(n_day)
    ]
    turned = lax.ppermute(white, AXES, turn)
    days = lax.all_gather(white, "day", axis=0)
    turned, days = lax.optimization_barrier((turned, days))
    pieces = jnp.broadcast_to(turned[None], (n_row * n_day,) + turned.shape)
    col_side = lax.all_to_all(pieces, ("row", "day"), 0, 0, tiled=True).reshape((n_row, n_day) + turned.shape)
    row_side = lax.all_gather(days, "col", axis=0)
    return stack(row_side, col_side)[None, None]


def solution(mesh):
    placed = (P("day", None, ("row", "col"), None), P("day", None, ("row", "col")))
    return jax.shard_map(
        body,
        mesh=mesh,
        in_specs=placed,
        out_specs=P("row", "col", None, "day", None),
        check_vma=False,
    )
```

```python
import math

import jax
import jax.numpy as jnp
import ml_dtypes
import numpy as np
from jax import lax
from jax.experimental import pallas as pl
from jax.experimental.pallas import tpu as pltpu
from jax.sharding import PartitionSpec as P

BINS = 256
LAGS = 128
HOURS = 6
AXES = ("row", "col", "day")
HOLDER = (
    (11, 10, 14, 9, 5, 2, 6, 8, 0, 3, 1, 15, 13, 7, 4, 12),
    (11, 10, 15, 8, 6, 4, 9, 7, 1, 2, 0, 3, 12, 14, 5, 13),
    (0, 9, 11, 8, 10, 12, 7, 4, 5, 3, 2, 1, 13, 6, 14, 15),
    (13, 0, 10, 9, 8, 11, 6, 4, 7, 1, 3, 2, 12, 5, 14, 15),
    (4, 0, 1, 3, 15, 14, 13, 10, 12, 11, 8, 2, 7, 5, 9, 6),
    (0, 1, 2, 3, 15, 14, 13, 11, 10, 12, 8, 7, 5, 6, 4, 9),
    (2, 5, 1, 3, 11, 15, 12, 13, 14, 8, 9, 0, 10, 4, 7, 6),
    (4, 3, 2, 0, 12, 15, 13, 14, 9, 10, 11, 8, 1, 5, 7, 6),
    (4, 8, 11, 9, 10, 1, 13, 6, 14, 2, 3, 15, 7, 0, 12, 5),
    (8, 5, 6, 4, 12, 1, 2, 0, 15, 3, 14, 7, 11, 13, 10, 9),
    (8, 6, 10, 9, 5, 7, 4, 2, 3, 1, 13, 12, 15, 0, 14, 11),
    (7, 10, 11, 8, 4, 6, 0, 3, 5, 2, 13, 1, 14, 12, 15, 9),
    (14, 2, 13, 3, 12, 15, 1, 0, 4, 8, 5, 9, 10, 6, 11, 7),
    (3, 9, 1, 0, 13, 12, 14, 2, 15, 8, 5, 4, 11, 7, 6, 10),
    (8, 5, 0, 9, 3, 1, 14, 13, 2, 15, 10, 12, 6, 7, 11, 4),
    (7, 10, 14, 13, 3, 0, 15, 12, 2, 1, 11, 8, 4, 9, 6, 5),
)
DT = jnp.bfloat16
G = 16
CH = 32
UN = 8
UC = 8


def lag_table():
    freq = (np.arange(BINS) + 0.5) * (math.pi / BINS)
    angles = freq[:, None] * (np.arange(LAGS) - LAGS // 2)[None, :]
    upper = np.concatenate([np.cos(angles), np.sin(angles)], 1)
    lower = np.concatenate([-np.sin(angles), np.cos(angles)], 1)
    return (np.concatenate([upper, lower], 0) / math.sqrt(HOURS * BINS)).astype(ml_dtypes.bfloat16)

def whiten_kernel(spec_ref, avail_ref, out_ref, rows):
    avail = avail_ref[0].astype(jnp.float32)
    for h in range(HOURS):
        x = spec_ref[0, h].astype(jnp.float32)
        re, im = x[:, :BINS], x[:, BINS:]
        power = re * re + im * im
        level = jnp.mean(power, axis=1, keepdims=True) + 1e-06
        factor = avail[:, h:h + 1] * lax.rsqrt(power + 0.09 * level)
        white = (re * factor, im * factor)
        for part in range(4):
            piece = white[part // 2][:, (part % 2) * 128:(part % 2) * 128 + 128]
            rows[pl.ds(part * 24 + h, 4, stride=6), :] = piece
    out_ref[...] = rows[...].astype(jnp.bfloat16)

def whiten(spectra, avail):
    return pl.pallas_call(
        whiten_kernel,
        out_shape=jax.ShapeDtypeStruct((96, 128), jnp.bfloat16),
        scratch_shapes=[pltpu.VMEM((96, 128), jnp.float32)],
        name="whiten",
    )(spectra, avail.transpose(0, 2, 1))

def tree(terms):
    while len(terms) > 1:
        terms = [terms[i] + terms[i + 1] if i + 1 < len(terms) else terms[i] for i in range(0, len(terms), 2)]
    return terms[0]


def stack_kernel(row_ref, col_ref, table_ref, out_ref, rows, firsts, seconds, cross):
    row_id, col_id, day_id = (lax.axis_index(name) for name in AXES)
    below = row_id > col_id
    above = row_id < col_id
    col_start = jnp.where(above, 8 * day_id, 8)
    corner = jnp.logical_and(row_id == col_id, day_id == 0)

    def held(shard):
        word = jnp.int32(0)
        for column in range(16):
            words = [np.uint32(sum(k << 4 * i for i, k in enumerate(HOLDER[column][at:at + 8]))).astype(np.int32) for at in (0, 8)]
            word = jnp.where(col_id == column, jnp.where(shard < 8, words[0], words[1]), word)
        return lax.shift_right_logical(word, 4 * (shard & 7)) & 15

    def split_hours(source):
        for day in range(2):
            for h in range(HOURS):
                for part in range(4):
                    v = rows[part, pl.ds(day * 192 + h, 32, stride=6), :]
                    if source == 1 and part >= 2:
                        v = -v
                    seconds[source, day, h, part] = v.astype(DT)

    @pl.loop(0, 8, unroll=2)
    def _(j):
        holder = held(col_start + j)
        for day in range(2):
            at = pl.ds(pl.multiple_of(day * 192 + j * 24, 8), 24)
            from_col = col_ref[holder, day]
            first = jnp.where(below, from_col, row_ref[j, day]).astype(jnp.float32)
            second = jnp.where(above, from_col, row_ref[j + 8 * day_id, day]).astype(jnp.float32)
            for part in range(4):
                firsts[part, at, :] = first[part * 24:part * 24 + 24]
                rows[part, at, :] = second[part * 24:part * 24 + 24]

    split_hours(0)

    @pl.when(corner)
    def _():
        @pl.loop(0, 8, unroll=2)
        def _(j):
            for day in range(2):
                at = pl.ds(pl.multiple_of(day * 192 + j * 24, 8), 24)
                first_at = pl.ds(pl.multiple_of(384 + day * 192 + j * 24, 8), 24)
                other = row_ref[j + 8, day].astype(jnp.float32)
                for part in range(4):
                    piece = other[part * 24:part * 24 + 24]
                    rows[part, at, :] = piece
                    firsts[part, first_at, :] = piece if part < 2 else -piece

        split_hours(1)

    def fill(a, plan):
        mark = lax.broadcasted_iota(jnp.int16, (G, 128), 0)
        inner = jnp.full((G, 128), lax.rem(a, G), jnp.int32).astype(jnp.int16)
        for day in range(2):
            parts = [[None] * 4 for _ in plan]
            for k in range(2):
                re, im = [[] for _ in plan], [[] for _ in plan]
                for h in range(HOURS):
                    at = day * 192 + a * 6 + h
                    wanted = sorted({s for p in plan for s in ((0, 1) if p is None else (p,))})
                    first = {
                        s: [
                            jnp.broadcast_to(firsts[part, pl.ds(s * 384 + at, 1), :], (G, 128)).astype(DT)
                            for part in (k, k + 2)
                        ]
                        for s in wanted
                    }
                    for q, p in enumerate(plan):
                        def second(s, part):
                            return seconds[s, day, h, part, q * G:(q + 1) * G, :]

                        if p is None:
                            fr, fi = (jnp.where(mark < inner, y, x) for x, y in zip(first[0], first[1]))
                            sr, si = (jnp.where(mark < inner, second(1, part), second(0, part)) for part in (k, k + 2))
                        else:
                            fr, fi = first[p]
                            sr, si = (second(p, part) for part in (k, k + 2))
                        re[q].append(fr * sr + fi * si)
                        im[q].append(fi * sr - fr * si)
                for q, p in enumerate(plan):
                    for part, terms in ((k, re[q]), (k + 2, im[q])):
                        total = tree(terms)
                        if p is None:
                            total = jnp.where(mark == inner, jnp.zeros_like(total), total)
                        at = pl.ds(pl.multiple_of(a * 32 + q * G, G), G)
                        cross[day, at, part * 128:part * 128 + 128] = total.astype(jnp.bfloat16)

    def finish(a):
        table = table_ref[...]
        lin = re = im = None
        for day in range(2):
            both = jnp.dot(cross[day], table, preferred_element_type=jnp.float32)
            corr, hilb = both[:, :LAGS], both[:, LAGS:]
            amp = corr * corr + hilb * hilb
            spread = jnp.sum(amp, axis=1, keepdims=True) * (0.01 / LAGS) + 1e-08
            inverse = lax.rsqrt(amp + spread)
            if day == 0:
                lin, re, im = corr, corr * inverse, hilb * inverse
            else:
                lin, re, im = lin + corr, re + corr * inverse, im + hilb * inverse
        stacked = (lin * (re * re + im * im) * 0.25).astype(jnp.bfloat16)
        out_ref[pl.ds(pl.multiple_of(a, CH), CH)] = stacked.reshape(CH, 32, LAGS)

    @pl.when(corner)
    def _():
        @pl.loop(0, G, unroll=UC)
        def _(a):
            fill(a, (None, 0))

        @pl.loop(G, 2 * G, unroll=UC)
        def _(a):
            fill(a, (1, None))

    @pl.when(jnp.logical_not(corner))
    def _():
        @pl.loop(0, 32, unroll=UN)
        def _(a):
            fill(a, (0, 0))

    finish(0)


def stack(row_side, col_side):
    vmem = pl.BlockSpec(memory_space=pltpu.VMEM)
    return pl.pallas_call(
        stack_kernel,
        in_specs=[vmem, vmem, vmem],
        out_specs=vmem,
        out_shape=jax.ShapeDtypeStruct((32, 32, LAGS), jnp.bfloat16),
        scratch_shapes=[
            pltpu.VMEM((4, 384, 128), jnp.float32),
            pltpu.VMEM((4, 768, 128), jnp.float32),
            pltpu.VMEM((2, 2, HOURS, 4, 32, 128), DT),
            pltpu.VMEM((2, CH * 32, 512), jnp.bfloat16),
        ],
        compiler_params=pltpu.CompilerParams(vmem_limit_bytes=32 * 1024 * 1024),
        name="stack",
    )(row_side, col_side, jnp.asarray(lag_table()))


def body(spectra, avail):
    n_row, n_col, n_day = (lax.axis_size(name) for name in AXES)
    white = whiten(spectra, avail)
    turn = [
        ((c * n_col + s) * n_day + day, (HOLDER[c][s] * n_col + c) * n_day + day)
        for c in range(n_row) for s in range(n_col) for day in range(n_day)
    ]
    turned = lax.ppermute(white, AXES, turn)
    days = lax.all_gather(white, "day", axis=0)
    turned, days = lax.optimization_barrier((turned, days))
    pieces = jnp.broadcast_to(turned[None], (n_row * n_day,) + turned.shape)
    col_side = lax.all_to_all(pieces, ("row", "day"), 0, 0, tiled=True).reshape((n_row, n_day) + turned.shape)
    row_side = lax.all_gather(days, "col", axis=0)
    return stack(row_side, col_side)[None, None]


def solution(mesh):
    placed = (P("day", None, ("row", "col"), None), P("day", None, ("row", "col")))
    return jax.shard_map(
        body,
        mesh=mesh,
        in_specs=placed,
        out_specs=P("row", "col", None, "day", None),
        check_vma=False,
    )
```

```python
import math

import jax
import jax.numpy as jnp
import ml_dtypes
import numpy as np
from jax import lax
from jax.experimental import pallas as pl
from jax.experimental.pallas import tpu as pltpu
from jax.sharding import PartitionSpec as P

BINS = 256
LAGS = 128
HOURS = 6
AXES = ("row", "col", "day")
HOLDER = (
    (11, 10, 9, 14, 6, 8, 7, 5, 4, 13, 0, 12, 2, 15, 1, 3),
    (10, 11, 9, 8, 6, 7, 4, 15, 0, 12, 1, 13, 5, 14, 2, 3),
    (10, 4, 11, 9, 12, 8, 15, 7, 6, 5, 2, 0, 13, 1, 3, 14),
    (8, 5, 10, 9, 13, 11, 14, 6, 7, 4, 3, 0, 15, 12, 2, 1),
    (12, 2, 15, 13, 10, 14, 9, 11, 6, 8, 1, 3, 4, 0, 7, 5),
    (8, 3, 12, 11, 15, 14, 10, 13, 9, 2, 0, 7, 4, 1, 5, 6),
    (1, 2, 0, 3, 9, 11, 15, 13, 12, 14, 8, 10, 7, 4, 6, 5),
    (3, 0, 2, 1, 12, 9, 14, 13, 10, 15, 11, 8, 6, 5, 7, 4),
    (4, 8, 12, 0, 3, 1, 2, 13, 14, 6, 10, 15, 11, 7, 9, 5),
    (5, 1, 4, 0, 2, 3, 12, 7, 14, 15, 11, 6, 10, 13, 9, 8),
    (6, 7, 5, 2, 1, 3, 4, 0, 15, 12, 8, 13, 11, 14, 10, 9),
    (0, 4, 3, 8, 12, 7, 2, 1, 6, 5, 15, 13, 9, 14, 11, 10),
    (4, 2, 3, 1, 0, 12, 15, 13, 8, 14, 5, 7, 10, 6, 9, 11),
    (5, 4, 12, 2, 1, 0, 13, 3, 8, 14, 6, 9, 11, 7, 10, 15),
    (4, 7, 5, 15, 0, 14, 2, 1, 3, 12, 13, 8, 9, 6, 10, 11),
    (6, 5, 7, 4, 2, 0, 3, 12, 15, 1, 14, 13, 8, 11, 10, 9),
)
DT = jnp.bfloat16
G = 16
CH = 32
UN = 8
UC = 8


def lag_table():
    freq = (np.arange(BINS) + 0.5) * (math.pi / BINS)
    angles = freq[:, None] * (np.arange(LAGS) - LAGS // 2)[None, :]
    upper = np.concatenate([np.cos(angles), np.sin(angles)], 1)
    lower = np.concatenate([-np.sin(angles), np.cos(angles)], 1)
    return (np.concatenate([upper, lower], 0) / math.sqrt(HOURS * BINS)).astype(ml_dtypes.bfloat16)

def whiten_kernel(spec_ref, avail_ref, out_ref, rows):
    avail = avail_ref[0].astype(jnp.float32)
    for h in range(HOURS):
        x = spec_ref[0, h].astype(jnp.float32)
        re, im = x[:, :BINS], x[:, BINS:]
        power = re * re + im * im
        level = jnp.mean(power, axis=1, keepdims=True) + 1e-06
        factor = avail[:, h:h + 1] * lax.rsqrt(power + 0.09 * level)
        white = (re * factor, im * factor)
        for part in range(4):
            piece = white[part // 2][:, (part % 2) * 128:(part % 2) * 128 + 128]
            rows[pl.ds(part * 24 + h, 4, stride=6), :] = piece
    out_ref[...] = rows[...].astype(jnp.bfloat16)

def whiten(spectra, avail):
    return pl.pallas_call(
        whiten_kernel,
        out_shape=jax.ShapeDtypeStruct((96, 128), jnp.bfloat16),
        scratch_shapes=[pltpu.VMEM((96, 128), jnp.float32)],
        compiler_params=pltpu.CompilerParams(vmem_limit_bytes=1048576),
        name="whiten",
    )(spectra, avail.transpose(0, 2, 1))

def tree(terms):
    while len(terms) > 1:
        terms = [terms[i] + terms[i + 1] if i + 1 < len(terms) else terms[i] for i in range(0, len(terms), 2)]
    return terms[0]


def stack_kernel(row_ref, col_ref, table_ref, out_ref, rows, firsts, seconds, cross):
    row_id, col_id, day_id = (lax.axis_index(name) for name in AXES)
    below = row_id > col_id
    above = row_id < col_id
    col_start = jnp.where(above, 8 * day_id, 8)
    corner = jnp.logical_and(row_id == col_id, day_id == 0)

    def held(shard):
        word = jnp.int32(0)
        for column in range(16):
            words = [np.uint32(sum(k << 4 * i for i, k in enumerate(HOLDER[column][at:at + 8]))).astype(np.int32) for at in (0, 8)]
            word = jnp.where(col_id == column, jnp.where(shard < 8, words[0], words[1]), word)
        return lax.shift_right_logical(word, 4 * (shard & 7)) & 15

    def split_hours(source):
        for day in range(2):
            for h in range(HOURS):
                for part in range(4):
                    v = rows[part, pl.ds(day * 192 + h, 32, stride=6), :]
                    if source == 1 and part >= 2:
                        v = -v
                    seconds[source, day, h, part] = v.astype(DT)

    @pl.loop(0, 8, unroll=2)
    def _(j):
        holder = held(col_start + j)
        for day in range(2):
            at = pl.ds(pl.multiple_of(day * 192 + j * 24, 8), 24)
            from_col = col_ref[holder, day]
            first = jnp.where(below, from_col, row_ref[j, day]).astype(jnp.float32)
            second = jnp.where(above, from_col, row_ref[j + 8 * day_id, day]).astype(jnp.float32)
            for part in range(4):
                firsts[part, at, :] = first[part * 24:part * 24 + 24]
                rows[part, at, :] = second[part * 24:part * 24 + 24]

    split_hours(0)

    @pl.when(corner)
    def _():
        @pl.loop(0, 8, unroll=2)
        def _(j):
            for day in range(2):
                at = pl.ds(pl.multiple_of(day * 192 + j * 24, 8), 24)
                first_at = pl.ds(pl.multiple_of(384 + day * 192 + j * 24, 8), 24)
                other = row_ref[j + 8, day].astype(jnp.float32)
                for part in range(4):
                    piece = other[part * 24:part * 24 + 24]
                    rows[part, at, :] = piece
                    firsts[part, first_at, :] = piece if part < 2 else -piece

        split_hours(1)

    def fill(a, plan):
        mark = lax.broadcasted_iota(jnp.int16, (G, 128), 0)
        inner = jnp.full((G, 128), lax.rem(a, G), jnp.int32).astype(jnp.int16)
        for day in range(2):
            parts = [[None] * 4 for _ in plan]
            for k in range(2):
                re, im = [[] for _ in plan], [[] for _ in plan]
                for h in range(HOURS):
                    at = day * 192 + a * 6 + h
                    wanted = sorted({s for p in plan for s in ((0, 1) if p is None else (p,))})
                    first = {
                        s: [
                            jnp.broadcast_to(firsts[part, pl.ds(s * 384 + at, 1), :], (G, 128)).astype(DT)
                            for part in (k, k + 2)
                        ]
                        for s in wanted
                    }
                    for q, p in enumerate(plan):
                        def second(s, part):
                            return seconds[s, day, h, part, q * G:(q + 1) * G, :]

                        if p is None:
                            fr, fi = (jnp.where(mark < inner, y, x) for x, y in zip(first[0], first[1]))
                            sr, si = (jnp.where(mark < inner, second(1, part), second(0, part)) for part in (k, k + 2))
                        else:
                            fr, fi = first[p]
                            sr, si = (second(p, part) for part in (k, k + 2))
                        re[q].append(fr * sr + fi * si)
                        im[q].append(fi * sr - fr * si)
                for q, p in enumerate(plan):
                    for part, terms in ((k, re[q]), (k + 2, im[q])):
                        total = tree(terms)
                        if p is None:
                            total = jnp.where(mark == inner, jnp.zeros_like(total), total)
                        at = pl.ds(pl.multiple_of(a * 32 + q * G, G), G)
                        cross[day, at, part * 128:part * 128 + 128] = total.astype(jnp.bfloat16)

    def finish(a):
        table = table_ref[...]
        lin = re = im = None
        for day in range(2):
            both = jnp.dot(cross[day], table, preferred_element_type=jnp.float32)
            corr, hilb = both[:, :LAGS], both[:, LAGS:]
            amp = corr * corr + hilb * hilb
            spread = jnp.sum(amp, axis=1, keepdims=True) * (0.01 / LAGS) + 1e-08
            inverse = lax.rsqrt(amp + spread)
            if day == 0:
                lin, re, im = corr, corr * inverse, hilb * inverse
            else:
                lin, re, im = lin + corr, re + corr * inverse, im + hilb * inverse
        stacked = (lin * (re * re + im * im) * 0.25).astype(jnp.bfloat16)
        out_ref[pl.ds(pl.multiple_of(a, CH), CH)] = stacked.reshape(CH, 32, LAGS)

    @pl.when(corner)
    def _():
        @pl.loop(0, G, unroll=UC)
        def _(a):
            fill(a, (None, 0))

        @pl.loop(G, 2 * G, unroll=UC)
        def _(a):
            fill(a, (1, None))

    @pl.when(jnp.logical_not(corner))
    def _():
        @pl.loop(0, 32, unroll=UN)
        def _(a):
            fill(a, (0, 0))

    finish(0)


def stack(row_side, col_side):
    vmem = pl.BlockSpec(memory_space=pltpu.VMEM)
    return pl.pallas_call(
        stack_kernel,
        in_specs=[vmem, vmem, vmem],
        out_specs=vmem,
        out_shape=jax.ShapeDtypeStruct((32, 32, LAGS), jnp.bfloat16),
        scratch_shapes=[
            pltpu.VMEM((4, 384, 128), jnp.float32),
            pltpu.VMEM((4, 768, 128), jnp.float32),
            pltpu.VMEM((2, 2, HOURS, 4, 32, 128), DT),
            pltpu.VMEM((2, CH * 32, 512), jnp.bfloat16),
        ],
        compiler_params=pltpu.CompilerParams(vmem_limit_bytes=32 * 1024 * 1024),
        name="stack",
    )(row_side, col_side, jnp.asarray(lag_table()))


def body(spectra, avail):
    n_row, n_col, n_day = (lax.axis_size(name) for name in AXES)
    white = whiten(spectra, avail)
    turn = [
        ((c * n_col + s) * n_day + day, (HOLDER[c][s] * n_col + c) * n_day + day)
        for c in range(n_row) for s in range(n_col) for day in range(n_day)
    ]
    turned = lax.ppermute(white, AXES, turn)
    days = lax.all_gather(white, "day", axis=0)
    turned, days = lax.optimization_barrier((turned, days))
    pieces = jnp.broadcast_to(turned[None], (n_row * n_day,) + turned.shape)
    col_side = lax.all_to_all(pieces, ("row", "day"), 0, 0, tiled=True).reshape((n_row, n_day) + turned.shape)
    row_side = lax.all_gather(days, "col", axis=0)
    return stack(row_side, col_side)[None, None]


def solution(mesh):
    placed = (P("day", None, ("row", "col"), None), P("day", None, ("row", "col")))
    return jax.shard_map(
        body,
        mesh=mesh,
        in_specs=placed,
        out_specs=P("row", "col", None, "day", None),
        check_vma=False,
    )
```

```python
import math

import jax
import jax.numpy as jnp
import ml_dtypes
import numpy as np
from jax import lax
from jax.experimental import pallas as pl
from jax.experimental.pallas import tpu as pltpu
from jax.sharding import PartitionSpec as P

BINS = 256
LAGS = 128
HOURS = 6
AXES = ("row", "col", "day")
HOLDER = (
    (10, 11, 14, 9, 6, 8, 13, 7, 3, 1, 0, 2, 5, 4, 12, 15),
    (10, 11, 8, 9, 7, 6, 4, 15, 1, 0, 12, 13, 3, 14, 2, 5),
    (10, 6, 11, 9, 8, 5, 15, 7, 4, 1, 3, 0, 13, 2, 14, 12),
    (11, 13, 10, 9, 8, 5, 6, 7, 4, 1, 3, 0, 12, 2, 14, 15),
    (12, 8, 13, 11, 10, 14, 9, 15, 2, 6, 3, 0, 1, 7, 5, 4),
    (2, 3, 10, 13, 15, 14, 11, 12, 7, 8, 0, 9, 1, 6, 4, 5),
    (3, 7, 0, 8, 15, 11, 13, 12, 10, 14, 1, 9, 2, 6, 4, 5),
    (2, 6, 0, 11, 9, 10, 13, 15, 14, 12, 8, 1, 5, 4, 7, 3),
    (8, 4, 5, 7, 3, 1, 13, 10, 6, 14, 2, 15, 11, 9, 0, 12),
    (5, 8, 0, 12, 2, 7, 6, 3, 15, 14, 11, 13, 10, 1, 9, 4),
    (6, 8, 10, 2, 1, 4, 3, 5, 7, 0, 14, 13, 12, 9, 11, 15),
    (7, 12, 11, 8, 3, 4, 0, 2, 13, 6, 15, 1, 14, 5, 10, 9),
    (14, 8, 3, 13, 12, 0, 2, 1, 4, 15, 5, 7, 6, 10, 9, 11),
    (8, 9, 2, 1, 0, 12, 3, 13, 4, 5, 10, 6, 7, 11, 15, 14),
    (4, 6, 14, 15, 13, 1, 2, 3, 12, 0, 5, 8, 7, 9, 11, 10),
    (13, 6, 8, 7, 2, 3, 12, 15, 14, 0, 1, 4, 5, 11, 9, 10),
)
DT = jnp.bfloat16
G = 16
CH = 32
UN = 8
UC = 8


def lag_table():
    freq = (np.arange(BINS) + 0.5) * (math.pi / BINS)
    angles = freq[:, None] * (np.arange(LAGS) - LAGS // 2)[None, :]
    upper = np.concatenate([np.cos(angles), np.sin(angles)], 1)
    lower = np.concatenate([-np.sin(angles), np.cos(angles)], 1)
    return (np.concatenate([upper, lower], 0) / math.sqrt(HOURS * BINS)).astype(ml_dtypes.bfloat16)

def whiten_kernel(spec_ref, avail_ref, out_ref, rows):
    avail = avail_ref[0].astype(jnp.float32)
    for h in range(HOURS):
        x = spec_ref[0, h].astype(jnp.float32)
        re, im = x[:, :BINS], x[:, BINS:]
        power = re * re + im * im
        level = jnp.mean(power, axis=1, keepdims=True) + 1e-06
        factor = avail[:, h:h + 1] * lax.rsqrt(power + 0.09 * level)
        white = (re * factor, im * factor)
        for part in range(4):
            piece = white[part // 2][:, (part % 2) * 128:(part % 2) * 128 + 128]
            rows[pl.ds(part * 24 + h, 4, stride=6), :] = piece
    out_ref[...] = rows[...].astype(jnp.bfloat16)

def whiten(spectra, avail):
    return pl.pallas_call(
        whiten_kernel,
        out_shape=jax.ShapeDtypeStruct((96, 128), jnp.bfloat16),
        scratch_shapes=[pltpu.VMEM((96, 128), jnp.float32)],
        compiler_params=pltpu.CompilerParams(vmem_limit_bytes=1048576),
        name="whiten",
    )(spectra, avail.transpose(0, 2, 1))

def tree(terms):
    while len(terms) > 1:
        terms = [terms[i] + terms[i + 1] if i + 1 < len(terms) else terms[i] for i in range(0, len(terms), 2)]
    return terms[0]


def stack_kernel(row_ref, col_ref, table_ref, out_ref, rows, firsts, seconds, cross):
    row_id, col_id, day_id = (lax.axis_index(name) for name in AXES)
    below = row_id > col_id
    above = row_id < col_id
    col_start = jnp.where(above, 8 * day_id, 8)
    corner = jnp.logical_and(row_id == col_id, day_id == 0)

    def held(shard):
        word = jnp.int32(0)
        for column in range(16):
            words = [np.uint32(sum(k << 4 * i for i, k in enumerate(HOLDER[column][at:at + 8]))).astype(np.int32) for at in (0, 8)]
            word = jnp.where(col_id == column, jnp.where(shard < 8, words[0], words[1]), word)
        return lax.shift_right_logical(word, 4 * (shard & 7)) & 15

    def split_hours(source):
        for day in range(2):
            for h in range(HOURS):
                for part in range(4):
                    v = rows[part, pl.ds(day * 192 + h, 32, stride=6), :]
                    if source == 1 and part >= 2:
                        v = -v
                    seconds[source, day, h, part] = v.astype(DT)

    @pl.loop(0, 8, unroll=2)
    def _(j):
        holder = held(col_start + j)
        for day in range(2):
            at = pl.ds(pl.multiple_of(day * 192 + j * 24, 8), 24)
            from_col = col_ref[holder, day]
            first = jnp.where(below, from_col, row_ref[j, day]).astype(jnp.float32)
            second = jnp.where(above, from_col, row_ref[j + 8 * day_id, day]).astype(jnp.float32)
            for part in range(4):
                firsts[part, at, :] = first[part * 24:part * 24 + 24]
                rows[part, at, :] = second[part * 24:part * 24 + 24]

    split_hours(0)

    @pl.when(corner)
    def _():
        @pl.loop(0, 8, unroll=2)
        def _(j):
            for day in range(2):
                at = pl.ds(pl.multiple_of(day * 192 + j * 24, 8), 24)
                first_at = pl.ds(pl.multiple_of(384 + day * 192 + j * 24, 8), 24)
                other = row_ref[j + 8, day].astype(jnp.float32)
                for part in range(4):
                    piece = other[part * 24:part * 24 + 24]
                    rows[part, at, :] = piece
                    firsts[part, first_at, :] = piece if part < 2 else -piece

        split_hours(1)

    def fill(a, plan):
        mark = lax.broadcasted_iota(jnp.int16, (G, 128), 0)
        inner = jnp.full((G, 128), lax.rem(a, G), jnp.int32).astype(jnp.int16)
        for day in range(2):
            parts = [[None] * 4 for _ in plan]
            for k in range(2):
                re, im = [[] for _ in plan], [[] for _ in plan]
                for h in range(HOURS):
                    at = day * 192 + a * 6 + h
                    wanted = sorted({s for p in plan for s in ((0, 1) if p is None else (p,))})
                    first = {
                        s: [
                            jnp.broadcast_to(firsts[part, pl.ds(s * 384 + at, 1), :], (G, 128)).astype(DT)
                            for part in (k, k + 2)
                        ]
                        for s in wanted
                    }
                    for q, p in enumerate(plan):
                        def second(s, part):
                            return seconds[s, day, h, part, q * G:(q + 1) * G, :]

                        if p is None:
                            fr, fi = (jnp.where(mark < inner, y, x) for x, y in zip(first[0], first[1]))
                            sr, si = (jnp.where(mark < inner, second(1, part), second(0, part)) for part in (k, k + 2))
                        else:
                            fr, fi = first[p]
                            sr, si = (second(p, part) for part in (k, k + 2))
                        re[q].append(fr * sr + fi * si)
                        im[q].append(fi * sr - fr * si)
                for q, p in enumerate(plan):
                    for part, terms in ((k, re[q]), (k + 2, im[q])):
                        total = tree(terms)
                        if p is None:
                            total = jnp.where(mark == inner, jnp.zeros_like(total), total)
                        at = pl.ds(pl.multiple_of(a * 32 + q * G, G), G)
                        cross[day, at, part * 128:part * 128 + 128] = total.astype(jnp.bfloat16)

    def finish(a):
        table = table_ref[...]
        lin = re = im = None
        for day in range(2):
            both = jnp.dot(cross[day], table, preferred_element_type=jnp.float32)
            corr, hilb = both[:, :LAGS], both[:, LAGS:]
            amp = corr * corr + hilb * hilb
            spread = jnp.sum(amp, axis=1, keepdims=True) * (0.01 / LAGS) + 1e-08
            inverse = lax.rsqrt(amp + spread)
            if day == 0:
                lin, re, im = corr, corr * inverse, hilb * inverse
            else:
                lin, re, im = lin + corr, re + corr * inverse, im + hilb * inverse
        stacked = (lin * (re * re + im * im) * 0.25).astype(jnp.bfloat16)
        out_ref[pl.ds(pl.multiple_of(a, CH), CH)] = stacked.reshape(CH, 32, LAGS)

    @pl.when(corner)
    def _():
        @pl.loop(0, G, unroll=UC)
        def _(a):
            fill(a, (None, 0))

        @pl.loop(G, 2 * G, unroll=UC)
        def _(a):
            fill(a, (1, None))

    @pl.when(jnp.logical_not(corner))
    def _():
        @pl.loop(0, 32, unroll=UN)
        def _(a):
            fill(a, (0, 0))

    finish(0)


def stack(row_side, col_side):
    vmem = pl.BlockSpec(memory_space=pltpu.VMEM)
    return pl.pallas_call(
        stack_kernel,
        in_specs=[vmem, vmem, vmem],
        out_specs=vmem,
        out_shape=jax.ShapeDtypeStruct((32, 32, LAGS), jnp.bfloat16),
        scratch_shapes=[
            pltpu.VMEM((4, 384, 128), jnp.float32),
            pltpu.VMEM((4, 768, 128), jnp.float32),
            pltpu.VMEM((2, 2, HOURS, 4, 32, 128), DT),
            pltpu.VMEM((2, CH * 32, 512), jnp.bfloat16),
        ],
        compiler_params=pltpu.CompilerParams(vmem_limit_bytes=32 * 1024 * 1024),
        name="stack",
    )(row_side, col_side, jnp.asarray(lag_table()))


def body(spectra, avail):
    n_row, n_col, n_day = (lax.axis_size(name) for name in AXES)
    white = whiten(spectra, avail)
    turn = [
        ((c * n_col + s) * n_day + day, (HOLDER[c][s] * n_col + c) * n_day + day)
        for c in range(n_row) for s in range(n_col) for day in range(n_day)
    ]
    turned = lax.ppermute(white, AXES, turn)
    days = lax.all_gather(white, "day", axis=0)
    turned, days = lax.optimization_barrier((turned, days))
    pieces = jnp.broadcast_to(turned[None], (n_row * n_day,) + turned.shape)
    col_side = lax.all_to_all(pieces, ("row", "day"), 0, 0, tiled=True).reshape((n_row, n_day) + turned.shape)
    row_side = lax.all_gather(days, "col", axis=0)
    return stack(row_side, col_side)[None, None]


def solution(mesh):
    placed = (P("day", None, ("row", "col"), None), P("day", None, ("row", "col")))
    return jax.shard_map(
        body,
        mesh=mesh,
        in_specs=placed,
        out_specs=P("row", "col", None, "day", None),
        check_vma=False,
    )
```

```python
import math

import jax
import jax.numpy as jnp
import ml_dtypes
import numpy as np
from jax import lax
from jax.experimental import pallas as pl
from jax.experimental.pallas import tpu as pltpu
from jax.sharding import PartitionSpec as P

BINS = 256
LAGS = 128
HOURS = 6
AXES = ("row", "col", "day")
HOLDER = (
    (10, 11, 14, 9, 6, 8, 13, 7, 3, 1, 0, 2, 5, 4, 12, 15),
    (10, 11, 8, 9, 7, 6, 4, 15, 1, 0, 12, 13, 3, 14, 2, 5),
    (10, 6, 11, 9, 8, 5, 15, 7, 4, 1, 3, 0, 13, 2, 14, 12),
    (11, 13, 10, 9, 8, 5, 6, 7, 4, 1, 3, 0, 12, 2, 14, 15),
    (12, 8, 13, 11, 10, 14, 9, 15, 2, 6, 3, 0, 1, 7, 5, 4),
    (2, 3, 10, 13, 15, 14, 11, 12, 7, 8, 0, 9, 1, 6, 4, 5),
    (3, 7, 0, 8, 15, 11, 13, 12, 10, 14, 1, 9, 2, 6, 4, 5),
    (2, 6, 0, 11, 9, 10, 13, 15, 14, 12, 8, 1, 5, 4, 7, 3),
    (8, 4, 5, 7, 3, 1, 13, 10, 6, 14, 2, 15, 11, 9, 0, 12),
    (5, 8, 0, 12, 2, 7, 6, 3, 15, 14, 11, 13, 10, 1, 9, 4),
    (6, 8, 10, 2, 1, 4, 3, 5, 7, 0, 14, 13, 12, 9, 11, 15),
    (7, 12, 11, 8, 3, 4, 0, 2, 13, 6, 15, 1, 14, 5, 10, 9),
    (14, 8, 3, 13, 12, 0, 2, 1, 4, 15, 5, 7, 6, 10, 9, 11),
    (8, 9, 2, 1, 0, 12, 3, 13, 4, 5, 10, 6, 7, 11, 15, 14),
    (4, 6, 14, 15, 13, 1, 2, 3, 12, 0, 5, 8, 7, 9, 11, 10),
    (13, 6, 8, 7, 2, 3, 12, 15, 14, 0, 1, 4, 5, 11, 9, 10),
)
DT = jnp.bfloat16
G = 16
CH = 32
UN = 8
UC = 8


def lag_table():
    freq = (np.arange(BINS) + 0.5) * (math.pi / BINS)
    angles = freq[:, None] * (np.arange(LAGS) - LAGS // 2)[None, :]
    upper = np.concatenate([np.cos(angles), np.sin(angles)], 1)
    lower = np.concatenate([-np.sin(angles), np.cos(angles)], 1)
    return (np.concatenate([upper, lower], 0) / math.sqrt(HOURS * BINS)).astype(ml_dtypes.bfloat16)

def whiten_kernel(spec_ref, avail_ref, out_ref, rows):
    avail = avail_ref[0].astype(jnp.float32)
    for h in range(HOURS):
        x = spec_ref[0, h].astype(jnp.float32)
        re, im = x[:, :BINS], x[:, BINS:]
        power = re * re + im * im
        level = jnp.mean(power, axis=1, keepdims=True) + 1e-06
        factor = avail[:, h:h + 1] * lax.rsqrt(power + 0.09 * level)
        white = (re * factor, im * factor)
        for part in range(4):
            piece = white[part // 2][:, (part % 2) * 128:(part % 2) * 128 + 128]
            rows[pl.ds(part * 24 + h, 4, stride=6), :] = piece
    out_ref[...] = rows[:96].astype(jnp.bfloat16)

def whiten(spectra, avail):
    return pl.pallas_call(
        whiten_kernel,
        out_shape=jax.ShapeDtypeStruct((96, 128), jnp.bfloat16),
        scratch_shapes=[pltpu.VMEM((128, 128), jnp.float32)],
        compiler_params=pltpu.CompilerParams(vmem_limit_bytes=1048576),
        name="whiten",
    )(spectra, avail.transpose(0, 2, 1))

def tree(terms):
    while len(terms) > 1:
        terms = [terms[i] + terms[i + 1] if i + 1 < len(terms) else terms[i] for i in range(0, len(terms), 2)]
    return terms[0]


def stack_kernel(row_ref, col_ref, table_ref, out_ref, rows, firsts, seconds, cross):
    row_id, col_id, day_id = (lax.axis_index(name) for name in AXES)
    below = row_id > col_id
    above = row_id < col_id
    col_start = jnp.where(above, 8 * day_id, 8)
    corner = jnp.logical_and(row_id == col_id, day_id == 0)

    def held(shard):
        word = jnp.int32(0)
        for column in range(16):
            words = [np.uint32(sum(k << 4 * i for i, k in enumerate(HOLDER[column][at:at + 8]))).astype(np.int32) for at in (0, 8)]
            word = jnp.where(col_id == column, jnp.where(shard < 8, words[0], words[1]), word)
        return lax.shift_right_logical(word, 4 * (shard & 7)) & 15

    def split_hours(source):
        for day in range(2):
            for h in range(HOURS):
                for part in range(4):
                    v = rows[part, pl.ds(day * 192 + h, 32, stride=6), :]
                    if source == 1 and part >= 2:
                        v = -v
                    seconds[source, day, h, part] = v.astype(DT)

    @pl.loop(0, 8, unroll=2)
    def _(j):
        holder = held(col_start + j)
        for day in range(2):
            at = pl.ds(pl.multiple_of(day * 192 + j * 24, 8), 24)
            from_col = col_ref[holder, day]
            first = jnp.where(below, from_col, row_ref[j, day]).astype(jnp.float32)
            second = jnp.where(above, from_col, row_ref[j + 8 * day_id, day]).astype(jnp.float32)
            for part in range(4):
                firsts[part, at, :] = first[part * 24:part * 24 + 24]
                rows[part, at, :] = second[part * 24:part * 24 + 24]

    split_hours(0)

    @pl.when(corner)
    def _():
        @pl.loop(0, 8, unroll=2)
        def _(j):
            for day in range(2):
                at = pl.ds(pl.multiple_of(day * 192 + j * 24, 8), 24)
                first_at = pl.ds(pl.multiple_of(384 + day * 192 + j * 24, 8), 24)
                other = row_ref[j + 8, day].astype(jnp.float32)
                for part in range(4):
                    piece = other[part * 24:part * 24 + 24]
                    rows[part, at, :] = piece
                    firsts[part, first_at, :] = piece if part < 2 else -piece

        split_hours(1)

    def fill(a, plan):
        mark = lax.broadcasted_iota(jnp.int16, (G, 128), 0)
        inner = jnp.full((G, 128), lax.rem(a, G), jnp.int32).astype(jnp.int16)
        for day in range(2):
            parts = [[None] * 4 for _ in plan]
            for k in range(2):
                re, im = [[] for _ in plan], [[] for _ in plan]
                for h in range(HOURS):
                    at = day * 192 + a * 6 + h
                    wanted = sorted({s for p in plan for s in ((0, 1) if p is None else (p,))})
                    first = {
                        s: [
                            jnp.broadcast_to(firsts[part, pl.ds(s * 384 + at, 1), :], (G, 128)).astype(DT)
                            for part in (k, k + 2)
                        ]
                        for s in wanted
                    }
                    for q, p in enumerate(plan):
                        def second(s, part):
                            return seconds[s, day, h, part, q * G:(q + 1) * G, :]

                        if p is None:
                            fr, fi = (jnp.where(mark < inner, y, x) for x, y in zip(first[0], first[1]))
                            sr, si = (jnp.where(mark < inner, second(1, part), second(0, part)) for part in (k, k + 2))
                        else:
                            fr, fi = first[p]
                            sr, si = (second(p, part) for part in (k, k + 2))
                        re[q].append(fr * sr + fi * si)
                        im[q].append(fi * sr - fr * si)
                for q, p in enumerate(plan):
                    for part, terms in ((k, re[q]), (k + 2, im[q])):
                        total = tree(terms)
                        if p is None:
                            total = jnp.where(mark == inner, jnp.zeros_like(total), total)
                        at = pl.ds(pl.multiple_of(a * 32 + q * G, G), G)
                        cross[day, at, part * 128:part * 128 + 128] = total.astype(jnp.bfloat16)

    def finish(a):
        table = table_ref[...]
        lin = re = im = None
        for day in range(2):
            both = jnp.dot(cross[day], table, preferred_element_type=jnp.float32)
            corr, hilb = both[:, :LAGS], both[:, LAGS:]
            amp = corr * corr + hilb * hilb
            spread = jnp.sum(amp, axis=1, keepdims=True) * (0.01 / LAGS) + 1e-08
            inverse = lax.rsqrt(amp + spread)
            if day == 0:
                lin, re, im = corr, corr * inverse, hilb * inverse
            else:
                lin, re, im = lin + corr, re + corr * inverse, im + hilb * inverse
        stacked = (lin * (re * re + im * im) * 0.25).astype(jnp.bfloat16)
        out_ref[pl.ds(pl.multiple_of(a, CH), CH)] = stacked.reshape(CH, 32, LAGS)

    @pl.when(corner)
    def _():
        @pl.loop(0, G, unroll=UC)
        def _(a):
            fill(a, (None, 0))

        @pl.loop(G, 2 * G, unroll=UC)
        def _(a):
            fill(a, (1, None))

    @pl.when(jnp.logical_not(corner))
    def _():
        @pl.loop(0, 32, unroll=UN)
        def _(a):
            fill(a, (0, 0))

    finish(0)


def stack(row_side, col_side):
    vmem = pl.BlockSpec(memory_space=pltpu.VMEM)
    return pl.pallas_call(
        stack_kernel,
        in_specs=[vmem, vmem, vmem],
        out_specs=vmem,
        out_shape=jax.ShapeDtypeStruct((32, 32, LAGS), jnp.bfloat16),
        scratch_shapes=[
            pltpu.VMEM((4, 392, 128), jnp.float32),
            pltpu.VMEM((4, 776, 128), jnp.float32),
            pltpu.VMEM((2, 2, HOURS, 4, 32, 128), DT),
            pltpu.VMEM((2, CH * 32, 512), jnp.bfloat16),
        ],
        compiler_params=pltpu.CompilerParams(vmem_limit_bytes=32 * 1024 * 1024),
        name="stack",
    )(row_side, col_side, jnp.asarray(lag_table()))


def body(spectra, avail):
    n_row, n_col, n_day = (lax.axis_size(name) for name in AXES)
    white = whiten(spectra, avail)
    turn = [
        ((c * n_col + s) * n_day + day, (HOLDER[c][s] * n_col + c) * n_day + day)
        for c in range(n_row) for s in range(n_col) for day in range(n_day)
    ]
    turned = lax.ppermute(white, AXES, turn)
    days = lax.all_gather(white, "day", axis=0)
    turned, days = lax.optimization_barrier((turned, days))
    pieces = jnp.broadcast_to(turned[None], (n_row * n_day,) + turned.shape)
    col_side = lax.all_to_all(pieces, ("row", "day"), 0, 0, tiled=True).reshape((n_row, n_day) + turned.shape)
    row_side = lax.all_gather(days, "col", axis=0)
    return stack(row_side, col_side)[None, None]


def solution(mesh):
    placed = (P("day", None, ("row", "col"), None), P("day", None, ("row", "col")))
    return jax.shard_map(
        body,
        mesh=mesh,
        in_specs=placed,
        out_specs=P("row", "col", None, "day", None),
        check_vma=False,
    )
```

```python
import math

import jax
import jax.numpy as jnp
import ml_dtypes
import numpy as np
from jax import lax
from jax.experimental import pallas as pl
from jax.experimental.pallas import tpu as pltpu
from jax.sharding import PartitionSpec as P

BINS = 256
LAGS = 128
HOURS = 6
AXES = ("row", "col", "day")
HOLDER = (
    (10, 11, 14, 9, 6, 8, 13, 7, 3, 1, 0, 2, 5, 4, 12, 15),
    (10, 11, 8, 9, 7, 6, 4, 15, 1, 0, 12, 13, 3, 14, 2, 5),
    (10, 6, 11, 9, 8, 5, 15, 7, 4, 1, 3, 0, 13, 2, 14, 12),
    (11, 13, 10, 9, 8, 5, 6, 7, 4, 1, 3, 0, 12, 2, 14, 15),
    (12, 8, 13, 11, 10, 14, 9, 15, 2, 6, 3, 0, 1, 7, 5, 4),
    (2, 3, 10, 13, 15, 14, 11, 12, 7, 8, 0, 9, 1, 6, 4, 5),
    (3, 7, 0, 8, 15, 11, 13, 12, 10, 14, 1, 9, 2, 6, 4, 5),
    (2, 6, 0, 11, 9, 10, 13, 15, 14, 12, 8, 1, 5, 4, 7, 3),
    (8, 4, 5, 7, 3, 1, 13, 10, 6, 14, 2, 15, 11, 9, 0, 12),
    (5, 8, 0, 12, 2, 7, 6, 3, 15, 14, 11, 13, 10, 1, 9, 4),
    (6, 8, 10, 2, 1, 4, 3, 5, 7, 0, 14, 13, 12, 9, 11, 15),
    (7, 12, 11, 8, 3, 4, 0, 2, 13, 6, 15, 1, 14, 5, 10, 9),
    (14, 8, 3, 13, 12, 0, 2, 1, 4, 15, 5, 7, 6, 10, 9, 11),
    (8, 9, 2, 1, 0, 12, 3, 13, 4, 5, 10, 6, 7, 11, 15, 14),
    (4, 6, 14, 15, 13, 1, 2, 3, 12, 0, 5, 8, 7, 9, 11, 10),
    (13, 6, 8, 7, 2, 3, 12, 15, 14, 0, 1, 4, 5, 11, 9, 10),
)
DT = jnp.bfloat16
G = 16
CH = 32
UN = 8
UC = 8


def lag_table():
    freq = (np.arange(BINS) + 0.5) * (math.pi / BINS)
    angles = freq[:, None] * (np.arange(LAGS) - LAGS // 2)[None, :]
    upper = np.concatenate([np.cos(angles), np.sin(angles)], 1)
    lower = np.concatenate([-np.sin(angles), np.cos(angles)], 1)
    return (np.concatenate([upper, lower], 0) / math.sqrt(HOURS * BINS)).astype(ml_dtypes.bfloat16)

def whiten_kernel(spec_ref, avail_ref, out_ref, rows):
    avail = avail_ref[0].astype(jnp.float32)
    for h in range(HOURS):
        x = spec_ref[0, h].astype(jnp.float32)
        re, im = x[:, :BINS], x[:, BINS:]
        power = re * re + im * im
        level = jnp.mean(power, axis=1, keepdims=True) + 1e-06
        factor = avail[:, h:h + 1] * lax.rsqrt(power + 0.09 * level)
        white = (re * factor, im * factor)
        for part in range(4):
            piece = white[part // 2][:, (part % 2) * 128:(part % 2) * 128 + 128]
            rows[pl.ds(part * 24 + h, 4, stride=6), :] = piece
    out_ref[...] = rows[:96].astype(jnp.bfloat16)

def whiten(spectra, avail):
    return pl.pallas_call(
        whiten_kernel,
        out_shape=jax.ShapeDtypeStruct((96, 128), jnp.bfloat16),
        scratch_shapes=[pltpu.VMEM((128, 128), jnp.float32)],
        compiler_params=pltpu.CompilerParams(vmem_limit_bytes=1048576),
        name="whiten",
    )(spectra, avail.transpose(0, 2, 1))

def tree(terms):
    while len(terms) > 1:
        terms = [terms[i] + terms[i + 1] if i + 1 < len(terms) else terms[i] for i in range(0, len(terms), 2)]
    return terms[0]


def stack_kernel(row_ref, col_ref, table_ref, out_ref, rows, firsts, seconds, cross):
    row_id, col_id, day_id = (lax.axis_index(name) for name in AXES)
    below = row_id > col_id
    above = row_id < col_id
    col_start = jnp.where(above, 8 * day_id, 8)
    corner = jnp.logical_and(row_id == col_id, day_id == 0)

    def held(shard):
        word = jnp.int32(0)
        for column in range(16):
            words = [np.uint32(sum(k << 4 * i for i, k in enumerate(HOLDER[column][at:at + 8]))).astype(np.int32) for at in (0, 8)]
            word = jnp.where(col_id == column, jnp.where(shard < 8, words[0], words[1]), word)
        return lax.shift_right_logical(word, 4 * (shard & 7)) & 15

    def split_hours(source):
        for day in range(2):
            for h in range(HOURS):
                for part in range(4):
                    v = rows[part, pl.ds(day * 192 + h, 32, stride=6), :]
                    if source == 1 and part >= 2:
                        v = -v
                    seconds[source, day, h, part] = v.astype(DT)

    @pl.loop(0, 8, unroll=8)
    def _(j):
        holder = held(col_start + j)
        for day in range(2):
            at = pl.ds(pl.multiple_of(day * 192 + j * 24, 8), 24)
            from_col = col_ref[holder, day]
            first = jnp.where(below, from_col, row_ref[j, day]).astype(jnp.float32)
            second = jnp.where(above, from_col, row_ref[j + 8 * day_id, day]).astype(jnp.float32)
            for part in range(4):
                firsts[part, at, :] = first[part * 24:part * 24 + 24]
                rows[part, at, :] = second[part * 24:part * 24 + 24]

    split_hours(0)

    @pl.when(corner)
    def _():
        @pl.loop(0, 8, unroll=8)
        def _(j):
            for day in range(2):
                at = pl.ds(pl.multiple_of(day * 192 + j * 24, 8), 24)
                first_at = pl.ds(pl.multiple_of(384 + day * 192 + j * 24, 8), 24)
                other = row_ref[j + 8, day].astype(jnp.float32)
                for part in range(4):
                    piece = other[part * 24:part * 24 + 24]
                    rows[part, at, :] = piece
                    firsts[part, first_at, :] = piece if part < 2 else -piece

        split_hours(1)

    def fill(a, plan):
        mark = lax.broadcasted_iota(jnp.int16, (G, 128), 0)
        inner = jnp.full((G, 128), lax.rem(a, G), jnp.int32).astype(jnp.int16)
        for day in range(2):
            parts = [[None] * 4 for _ in plan]
            for k in range(2):
                re, im = [[] for _ in plan], [[] for _ in plan]
                for h in range(HOURS):
                    at = day * 192 + a * 6 + h
                    wanted = sorted({s for p in plan for s in ((0, 1) if p is None else (p,))})
                    first = {
                        s: [
                            jnp.broadcast_to(firsts[part, pl.ds(s * 384 + at, 1), :], (G, 128)).astype(DT)
                            for part in (k, k + 2)
                        ]
                        for s in wanted
                    }
                    for q, p in enumerate(plan):
                        def second(s, part):
                            return seconds[s, day, h, part, q * G:(q + 1) * G, :]

                        if p is None:
                            fr, fi = (jnp.where(mark < inner, y, x) for x, y in zip(first[0], first[1]))
                            sr, si = (jnp.where(mark < inner, second(1, part), second(0, part)) for part in (k, k + 2))
                        else:
                            fr, fi = first[p]
                            sr, si = (second(p, part) for part in (k, k + 2))
                        re[q].append(fr * sr + fi * si)
                        im[q].append(fi * sr - fr * si)
                for q, p in enumerate(plan):
                    for part, terms in ((k, re[q]), (k + 2, im[q])):
                        total = tree(terms)
                        if p is None:
                            total = jnp.where(mark == inner, jnp.zeros_like(total), total)
                        at = pl.ds(pl.multiple_of(a * 32 + q * G, G), G)
                        cross[day, at, part * 128:part * 128 + 128] = total.astype(jnp.bfloat16)

    def finish(a):
        table = table_ref[...]
        lin = re = im = None
        for day in range(2):
            both = jnp.dot(cross[day], table, preferred_element_type=jnp.float32)
            corr, hilb = both[:, :LAGS], both[:, LAGS:]
            amp = corr * corr + hilb * hilb
            spread = jnp.sum(amp, axis=1, keepdims=True) * (0.01 / LAGS) + 1e-08
            inverse = lax.rsqrt(amp + spread)
            if day == 0:
                lin, re, im = corr, corr * inverse, hilb * inverse
            else:
                lin, re, im = lin + corr, re + corr * inverse, im + hilb * inverse
        stacked = (lin * (re * re + im * im) * 0.25).astype(jnp.bfloat16)
        out_ref[pl.ds(pl.multiple_of(a, CH), CH)] = stacked.reshape(CH, 32, LAGS)

    @pl.when(corner)
    def _():
        @pl.loop(0, G, unroll=UC)
        def _(a):
            fill(a, (None, 0))

        @pl.loop(G, 2 * G, unroll=UC)
        def _(a):
            fill(a, (1, None))

    @pl.when(jnp.logical_not(corner))
    def _():
        @pl.loop(0, 32, unroll=UN)
        def _(a):
            fill(a, (0, 0))

    finish(0)


def stack(row_side, col_side):
    vmem = pl.BlockSpec(memory_space=pltpu.VMEM)
    return pl.pallas_call(
        stack_kernel,
        in_specs=[vmem, vmem, vmem],
        out_specs=vmem,
        out_shape=jax.ShapeDtypeStruct((32, 32, LAGS), jnp.bfloat16),
        scratch_shapes=[
            pltpu.VMEM((4, 392, 128), jnp.float32),
            pltpu.VMEM((4, 776, 128), jnp.float32),
            pltpu.VMEM((2, 2, HOURS, 4, 32, 128), DT),
            pltpu.VMEM((2, CH * 32, 512), jnp.bfloat16),
        ],
        compiler_params=pltpu.CompilerParams(vmem_limit_bytes=32 * 1024 * 1024),
        name="stack",
    )(row_side, col_side, jnp.asarray(lag_table()))


def body(spectra, avail):
    n_row, n_col, n_day = (lax.axis_size(name) for name in AXES)
    white = whiten(spectra, avail)
    turn = [
        ((c * n_col + s) * n_day + day, (HOLDER[c][s] * n_col + c) * n_day + day)
        for c in range(n_row) for s in range(n_col) for day in range(n_day)
    ]
    turned = lax.ppermute(white, AXES, turn)
    days = lax.all_gather(white, "day", axis=0)
    turned, days = lax.optimization_barrier((turned, days))
    pieces = jnp.broadcast_to(turned[None], (n_row * n_day,) + turned.shape)
    col_side = lax.all_to_all(pieces, ("row", "day"), 0, 0, tiled=True).reshape((n_row, n_day) + turned.shape)
    row_side = lax.all_gather(days, "col", axis=0)
    return stack(row_side, col_side)[None, None]


def solution(mesh):
    placed = (P("day", None, ("row", "col"), None), P("day", None, ("row", "col")))
    return jax.shard_map(
        body,
        mesh=mesh,
        in_specs=placed,
        out_specs=P("row", "col", None, "day", None),
        check_vma=False,
    )
```
